256 devices in a mesh: seq: 128 (over y_hi, x, z, core), chan: 2 (over y_lo).
Axes of the slice: x: 4, y: 4 (y_hi: 2, y_lo: 2; y = y_hi * 2 + y_lo), z: 8, core: 2. Of those that a mesh axis runs over, the one named last changes fastest.
Arguments:
- inputs: bfloat16 [32768, 2048], P(('seq', 'chan')), may hold values from -6 to 6
- cotangent: bfloat16 [32768, 2048], P(('seq', 'chan')), may hold values from -6 to 6
- filter_spec: bfloat16 [2, 256, 128, 2048], P(None, 'seq', None, 'chan'), may hold values from -6 to 6
Outputs:
- grad_input: bfloat16 [32768, 2048], P(('seq', 'chan'))
- grad_filter: bfloat16 [2, 256, 128, 2048], P(None, 'seq', None, 'chan')
The draws below stay inside these ranges and needn't reach their ends.
All inputs are finite; a program needn't handle non-finite values.
Results may differ from the reference program's by a relative error of at most 0.001.
Values may be sent and summed in bfloat16 or wider, within the bound.
A program may use at most 128 MiB of HBM per device.

```python
import math
import jax
import jax.numpy as jnp
from jax import lax

C = 2048
LENGTH = 32768
SLOTS = 256
HALF = 128


def levels(rng, extent, shards, low, top_value):
    factor_of = 1.0
    for axis_at, shards_of in shards:
        draws = jax.random.uniform(jax.random.fold_in(jax.random.fold_in(rng, 6), axis_at), (shards_of,), jnp.float32, low / len(shards), top_value / len(shards))
        factor_of = factor_of * jnp.repeat(jnp.exp(draws), extent[axis_at] // shards_of).reshape((-1,) + (1,) * (len(extent) - 1 - axis_at))
    return factor_of


def normal_values(own_key, shape, spread, bound, shards=(), kind=jnp.bfloat16):
    result = spread * jax.random.normal(own_key, shape, jnp.float32)
    if shards:
        result = result * levels(own_key, shape, shards, -0.22, 0.18)
    return jnp.clip(result, -bound, bound).astype(kind)


def setup_inputs(seed: int = 0) -> dict:
    key_of = jax.random.split(jax.random.key(seed), 4)
    return {
        "inputs": normal_values(key_of[0], (LENGTH, C), 1.0, 6.0, ((0, 256),)),
        "cotangent": normal_values(key_of[1], (LENGTH, C), 1.0, 6.0, ((0, 256),)),
        "filter_spec": normal_values(key_of[2], (2, SLOTS, HALF, C), 1.0, 6.0, ((1, 128), (3, 2))),
    }


def class_of(slot_ids, slot_count):
    halved = slot_ids // 2
    return jnp.where(slot_ids % 2 == 0, halved, jnp.where(slot_ids == 1, slot_count // 2, slot_count - halved))


def reference(inputs, cotangent, filter_spec):
    points = 2 * LENGTH
    group = math.gcd(C, 128)
    blocks = C // group
    slot_ids = jnp.arange(SLOTS, dtype=jnp.int32)
    bin_index = (class_of(slot_ids, SLOTS)[:, None] + SLOTS * jnp.arange(HALF, dtype=jnp.int32)[None, :]).reshape(-1)

    def one_group(parts):
        input_part, cotangent_part, filter_part = parts
        input_spec = jnp.fft.rfft(input_part.astype(jnp.float32), n=points, axis=0)
        cotangent_spec = jnp.fft.rfft(cotangent_part.astype(jnp.float32), n=points, axis=0)
        filter_re = filter_part[0].astype(jnp.float32).reshape(SLOTS * HALF, group)
        filter_im = filter_part[1].astype(jnp.float32).reshape(SLOTS * HALF, group)
        zero_rows = jnp.zeros((LENGTH + 1, group), jnp.float32)
        full_re = zero_rows.at[bin_index].set(filter_re)
        full_im = zero_rows.at[bin_index].set(filter_im)
        full_re = full_re.at[LENGTH].set(filter_im[0])
        full_im = full_im.at[0].set(0.0)
        spectrum = full_re + 1j * full_im
        weighted = jnp.conj(spectrum) * cotangent_spec
        grad_part = jnp.fft.irfft(weighted, n=points, axis=0)[:LENGTH]
        cross = input_spec * jnp.conj(cotangent_spec)
        picked = cross[bin_index]
        grad_re = (2.0 / points) * jnp.real(picked)
        grad_im = -(2.0 / points) * jnp.imag(picked)
        grad_re = grad_re.at[0].set(jnp.real(cross[0]) / points)
        grad_im = grad_im.at[0].set(jnp.real(cross[LENGTH]) / points)
        stacked = jnp.stack([grad_re, grad_im]).reshape(2, SLOTS, HALF, group)
        return grad_part.astype(jnp.bfloat16), stacked.astype(jnp.bfloat16)

    input_groups = inputs.reshape(LENGTH, blocks, group).transpose(1, 0, 2)
    cotangent_groups = cotangent.reshape(LENGTH, blocks, group).transpose(1, 0, 2)
    filter_groups = filter_spec.reshape(2, SLOTS, HALF, blocks, group).transpose(3, 0, 1, 2, 4)
    grad_groups, filter_grads = lax.map(one_group, (input_groups, cotangent_groups, filter_groups))
    grad_input = grad_groups.transpose(1, 0, 2).reshape(LENGTH, C)
    grad_filter = filter_grads.transpose(1, 2, 3, 0, 4).reshape(2, SLOTS, HALF, C)
    return (grad_input, grad_filter)
```

```python
import functools

import jax
import jax.numpy as jnp
import ml_dtypes
import numpy as np
from jax import lax
from jax.experimental import pallas as pl
from jax.experimental.pallas import tpu as pltpu
from jax.sharding import PartitionSpec as P

MESH = pl.DeviceIdType.MESH
OWN = 8
LANES = 128
F32 = jnp.float32
BF16 = jnp.bfloat16


def split(table):
    high = table.astype(ml_dtypes.bfloat16)
    low = (table - high.astype(np.float64)).astype(ml_dtypes.bfloat16)
    return high, low


def angles(left, right, modulus):
    return 2.0 * np.pi * (np.outer(left, right) % modulus) / modulus


@functools.cache
def tables(shards, width):
    classes, offsets = 2 * shards, 2 * width
    points = classes * offsets
    c = np.arange(shards)
    p = np.arange(shards)
    j = np.arange(offsets)
    r = np.arange(width)
    turn = angles(c, p, classes)
    first = np.concatenate([np.cos(turn), -np.sin(turn)])
    first[shards] = np.cos(np.pi * p)
    last = np.concatenate([2.0 * np.cos(turn.T), -2.0 * np.sin(turn.T)], axis=1)
    last[:, 0] = 1.0
    last[:, shards] = np.cos(np.pi * p)
    twist = angles(np.arange(shards + 1), j, points)
    twist_cos, twist_sin = np.cos(twist), -np.sin(twist)
    low, up = angles(j, r, offsets), angles(j, r + 1, offsets)
    inner = np.block(
        [
            [np.cos(low), -np.sin(low), np.cos(up), -np.sin(up)],
            [np.sin(low), np.cos(low), -np.sin(up), -np.cos(up)],
        ]
    )
    edge = np.stack([twist_cos[shards], twist_sin[shards]] + [np.zeros(offsets)] * 6)
    first_high, first_low = split(first)
    last_high, last_low = split(last)
    inner_high, inner_low = split(inner)
    return (
        np.concatenate([first_high, first_low], axis=1),
        np.concatenate([last_high, last_low], axis=0),
        np.stack([inner_high, inner_low]),
        np.stack([inner_high.T, inner_low.T]),
        np.stack([twist_cos[:shards], twist_sin[:shards]]).astype(np.float32),
        edge.astype(np.float32),
    )


def halves(value):
    high = value.astype(BF16)
    return high, (value - high.astype(F32)).astype(BF16)


def dot(left, right):
    return jnp.dot(left, right, preferred_element_type=F32)


def dot3(left_high, left_low, right_ref):
    return (
        dot(left_high, right_ref[0]) + dot(left_high, right_ref[1]) + dot(left_low, right_ref[0])
    )


def kernel(
    shards,
    x_hbm,
    ct_hbm,
    f_hbm,
    first_hbm,
    last_hbm,
    inner_hbm,
    outer_hbm,
    twist_hbm,
    edge_hbm,
    gi_hbm,
    gf_hbm,
    x_v,
    f_v,
    first,
    last,
    inner,
    outer,
    twist,
    edge,
    x_out,
    x_got,
    f_out,
    f_got,
    g_out,
    g_got,
    y_out,
    y_got,
    wide,
    z_high,
    z_low,
    spec,
    f_wide,
    g_wide,
    w_high,
    w_low,
    back,
    y_wide,
    gi_v,
    gf_v,
    load_sem,
    send_sem,
    recv_sem,
    store_sem,
):
    width = LANES
    all_devices = 2 * shards
    points = 4 * shards * width
    both = 2 * OWN
    s, h = lax.axis_index("seq"), lax.axis_index("chan")
    me = 2 * s + h
    own = h * shards + s

    loads = [
        pltpu.make_async_copy(source, target, load_sem.at[at])
        for at, (source, target) in enumerate(
            (
                (x_hbm, x_v.at[0]),
                (ct_hbm, x_v.at[1]),
                (f_hbm, f_v),
                (first_hbm, first),
                (last_hbm, last),
                (inner_hbm, inner),
                (outer_hbm, outer),
                (twist_hbm, twist),
                (edge_hbm, edge),
            )
        )
    ]
    for load in loads:
        load.start()

    barrier = pltpu.get_barrier_semaphore()

    def greet(k, carry):
        t = (me + k) % all_devices
        pl.semaphore_signal(barrier, inc=1, device_id=(t // 2, t % 2), device_id_type=MESH)
        return carry

    lax.fori_loop(1, all_devices, greet, 0)

    def remote(phase, source, target, device):
        return pltpu.make_async_remote_copy(
            src_ref=source,
            dst_ref=target,
            send_sem=send_sem.at[phase],
            recv_sem=recv_sem.at[phase],
            device_id=device,
            device_id_type=MESH,
        )

    def to_all(phase, out, got):
        def send(k, carry):
            t = (me + k) % all_devices
            remote(phase, out.at[t % 2 * shards + t // 2], got.at[own], (t // 2, t % 2)).start()
            return carry

        lax.fori_loop(1, all_devices, send, 0)

    def to_row(phase, out, got):
        def send(k, carry):
            t = (s + k) % shards
            remote(phase, out.at[t], got.at[s], (t, h)).start()
            return carry

        lax.fori_loop(1, shards, send, 0)

    def whole(phase, out, got, count):
        rest = pl.ds(0, count - 1)
        return remote(phase, out.at[rest], got.at[rest], ((s + 1) % shards, h))

    loads[0].wait()
    loads[1].wait()

    def turn_x(t, carry):
        at = pl.ds(pl.multiple_of(t * LANES, LANES), LANES)
        parts = [x_v[a, :, at].astype(F32).T.reshape(LANES // OWN, OWN, width) for a in range(2)]
        x_out[pl.ds(t * (LANES // OWN), LANES // OWN)] = jnp.concatenate(parts, axis=1).astype(BF16)
        return carry

    lax.fori_loop(0, all_devices * OWN // LANES, turn_x, 0)
    x_got[own] = x_out[own]
    pl.semaphore_wait(barrier, all_devices - 1)
    to_all(0, x_out, x_got)

    loads[2].wait()

    def turn_f(t, carry):
        at = pl.ds(pl.multiple_of(t * LANES, LANES), LANES)
        for g in range(2):
            parts = [
                f_v[part, g, :, at].astype(F32).T.reshape(LANES // OWN, OWN, width)
                for part in range(2)
            ]
            f_out[pl.ds(t * (LANES // OWN), LANES // OWN), g] = jnp.concatenate(
                parts, axis=1
            ).astype(BF16)
        return carry

    lax.fori_loop(0, shards * OWN // LANES, turn_f, 0)
    f_got[s] = f_out[s]
    to_row(1, f_out, f_got)
    for load in loads[3:]:
        load.wait()

    whole(0, x_out, x_got, all_devices).wait_recv()

    def widen_x(t, carry):
        rows = pl.ds(pl.multiple_of(t * 16 * both, 16 * both), 16 * both)
        wide[rows] = x_got[pl.ds(t * 16, 16)].astype(F32).reshape(16 * both, width)
        return carry

    lax.fori_loop(0, all_devices // 16, widen_x, 0)

    def forward_first(q, carry):
        x = jnp.concatenate(
            [wide[pl.ds(a * shards * both + q, shards, stride=both), :] for a in range(2)], axis=1
        ).astype(BF16)
        y = dot(first[...], jnp.concatenate([x, x], axis=0))
        real, imag = y[:shards], y[shards:]
        alone = imag[0:1]
        zero_row = lax.broadcasted_iota(jnp.int32, imag.shape, 0) == 0
        imag = jnp.where(zero_row, 0.0, imag)
        z = jnp.concatenate(
            [real * twist[0] - imag * twist[1], real * twist[1] + imag * twist[0]], axis=1
        )
        rows = pl.ds(pl.multiple_of(q * shards, shards), shards)
        high, low = halves(z)
        z_high[rows] = high
        z_low[rows] = low
        spec[pl.ds(both * shards + q, 1), :] = jnp.concatenate(
            [alone * edge[0:1], alone * edge[1:2]], axis=1
        )
        return carry

    lax.fori_loop(0, both, forward_first, 0)
    tail = pl.ds(both * shards, both)
    high, low = halves(spec[tail])
    z_high[tail] = high
    z_low[tail] = low

    rows_forward = z_high.shape[0]
    step_forward = rows_forward // 3 if rows_forward % 48 == 0 else rows_forward

    def forward_second(t, carry):
        rows = pl.ds(pl.multiple_of(t * step_forward, 16), step_forward)
        spec[rows] = dot3(z_high[rows], z_low[rows], inner)
        return carry

    lax.fori_loop(0, rows_forward // step_forward, forward_second, 0)

    for q in range(both):
        zero, extra = pl.ds(q * shards, 1), pl.ds(both * shards + q, 1)
        kept = spec[zero, 2 * width : 3 * width]
        spec[zero, 2 * width :] = spec[extra, : 2 * width]
        spec[extra, 2 * width : 3 * width] = kept

    corner = (lax.broadcasted_iota(jnp.int32, (shards, width), 0) == 0) & (
        lax.broadcasted_iota(jnp.int32, (shards, width), 1) == 0
    )

    def spectrum(q, g):
        rows = pl.ds(pl.multiple_of(q * shards, shards), shards)
        at = 2 * width * g
        return spec[rows, at : at + width], spec[rows, at + width : at + 2 * width]

    def top(q):
        return spec[pl.ds(both * shards + q, 1), 3 * width - 1 : 3 * width]

    for ch in range(OWN):
        for g in range(2):
            (ur, ui), (vr, vi) = spectrum(ch, g), spectrum(OWN + ch, g)
            real = (ur * vr + ui * vi) * (2.0 / points)
            imag = (ur * vi - ui * vr) * (2.0 / points)
            if g == 0:
                real = jnp.where(corner, 0.5 * real, real)
                imag = jnp.where(corner, top(ch) * top(OWN + ch) * (1.0 / points), imag)
            g_wide[g, pl.ds(ch, shards, stride=both), :] = real
            g_wide[g, pl.ds(OWN + ch, shards, stride=both), :] = imag

    def narrow_g(t, carry):
        rows = pl.ds(pl.multiple_of(t * 16 * both, 16 * both), 16 * both)
        for g in range(2):
            g_out[pl.ds(t * 16, 16), g] = g_wide[g, rows].reshape(16, both, width).astype(BF16)
        return carry

    lax.fori_loop(0, shards // 16, narrow_g, 0)
    g_got[s] = g_out[s]
    to_row(2, g_out, g_got)

    whole(1, f_out, f_got, shards).wait_recv()

    def widen_f(t, carry):
        rows = pl.ds(pl.multiple_of(t * 16 * both, 16 * both), 16 * both)
        for g in range(2):
            f_wide[g, rows] = f_got[pl.ds(t * 16, 16), g].astype(F32).reshape(16 * both, width)
        return carry

    lax.fori_loop(0, shards // 16, widen_f, 0)

    row_at = lax.broadcasted_iota(jnp.int32, (shards, width), 0)
    lane_at = lax.broadcasted_iota(jnp.int32, (shards, width), 1)
    lane_one = lax.broadcasted_iota(jnp.int32, (1, width), 1)
    extra_rows = w_high.shape[0] - OWN * shards
    back[pl.ds(OWN * shards, extra_rows)] = jnp.zeros((extra_rows, 4 * width), F32)
    for ch in range(OWN):
        fields = []
        for g in range(2):
            vr, vi = spectrum(OWN + ch, g)
            fr = f_wide[g, pl.ds(ch, shards, stride=both), :]
            fi = f_wide[g, pl.ds(OWN + ch, shards, stride=both), :]
            if g == 0:
                above = top(OWN + ch) * fi[0:1, 0:1]
                fi = jnp.where(corner, 0.0, fi)
            fields.append((fr * vr + fi * vi, fr * vi - fi * vr))
        (ar, ai), (br, bi) = fields
        back[pl.ds(OWN * shards + ch, 1), : 2 * width] = 2.0 * jnp.concatenate(
            [br[0:1], bi[0:1]], axis=1
        )
        twice = (row_at == 0) & (lane_at > 0)
        ar = jnp.where(twice, 2.0 * ar, ar)
        ai = jnp.where(twice, 2.0 * ai, jnp.where(corner, 0.0, ai))
        br = jnp.where(row_at == 0, jnp.where(lane_one == width - 1, above, 0.0), br)
        bi = jnp.where(row_at == 0, 0.0, bi)
        high, low = halves(jnp.concatenate([ar, ai, br, bi], axis=1))
        rows = pl.ds(ch * shards, shards)
        w_high[rows] = high
        w_low[rows] = low
    tail_back = pl.ds(OWN * shards, extra_rows)
    high, low = halves(back[tail_back])
    w_high[tail_back] = high
    w_low[tail_back] = low

    rows_back = w_high.shape[0]
    step_back = rows_back // 3 if rows_back % 48 == 0 else rows_back

    def inverse_first(t, carry):
        rows = pl.ds(pl.multiple_of(t * step_back, 16), step_back)
        back[rows] = dot3(w_high[rows], w_low[rows], outer)
        return carry

    lax.fori_loop(0, rows_back // step_back, inverse_first, 0)

    for ch in range(OWN):
        rows = pl.ds(ch * shards, shards)
        hr, hi = back[rows, : 2 * width], back[rows, 2 * width :]
        extra = pl.ds(OWN * shards + ch, 1)
        er, ei = back[extra, : 2 * width], back[extra, 2 * width :]
        kr = hr * twist[0] + hi * twist[1]
        ki = hi * twist[0] - hr * twist[1]
        zero_row = lax.broadcasted_iota(jnp.int32, ki.shape, 0) == 0
        ki = jnp.where(zero_row, er * edge[0:1] + ei * edge[1:2], ki)
        high, low = halves(jnp.concatenate([kr, ki], axis=0))
        main = dot(last[...], high)
        y = main[:shards] + main[shards:] + dot(last[pl.ds(0, shards)], low)
        y = y * (1.0 / points)
        for a in range(2):
            y_wide[a, pl.ds(ch, shards, stride=OWN), :] = y[:, a * width : (a + 1) * width]

    def narrow_y(t, carry):
        rows = pl.ds(pl.multiple_of(t * 16 * OWN, 16 * OWN), 16 * OWN)
        for a in range(2):
            y_out[pl.ds(a * shards + t * 16, 16)] = (
                y_wide[a, rows].reshape(16, OWN, width).astype(BF16)
            )
        return carry

    lax.fori_loop(0, shards // 16, narrow_y, 0)
    y_got[own] = y_out[own]
    to_all(3, y_out, y_got)

    whole(2, g_out, g_got, shards).wait_recv()

    def turn_g(t, carry):
        at = pl.ds(pl.multiple_of(t * LANES, LANES), LANES)
        for g in range(2):
            block = g_got[pl.ds(t * (LANES // OWN), LANES // OWN), g].astype(F32)
            for part in range(2):
                rows = block[:, part * OWN : (part + 1) * OWN].reshape(LANES, width)
                gf_v[part, g, :, at] = rows.T.astype(BF16)
        return carry

    lax.fori_loop(0, shards * OWN // LANES, turn_g, 0)
    store_gf = pltpu.make_async_copy(gf_v, gf_hbm, store_sem.at[0])
    store_gf.start()

    whole(3, y_out, y_got, all_devices).wait_recv()

    def turn_y(t, carry):
        at = pl.ds(pl.multiple_of(t * LANES, LANES), LANES)
        rows = y_got[pl.ds(t * (LANES // OWN), LANES // OWN)].astype(F32).reshape(LANES, width)
        gi_v[:, at] = rows.T.astype(BF16)
        return carry

    lax.fori_loop(0, all_devices * OWN // LANES, turn_y, 0)
    store_gi = pltpu.make_async_copy(gi_v, gi_hbm, store_sem.at[1])
    store_gi.start()

    whole(0, x_out, x_got, all_devices).wait_send()
    whole(1, f_out, f_got, shards).wait_send()
    whole(2, g_out, g_got, shards).wait_send()
    whole(3, y_out, y_got, all_devices).wait_send()
    store_gf.wait()
    store_gi.wait()


def local(inputs, cotangent, filter_spec):
    width, channels = inputs.shape
    shards = lax.axis_size("seq")
    group = channels // 2
    both = 2 * OWN
    constants = [jnp.asarray(table) for table in tables(shards, width)]
    extra = 32
    scratch = [
        ((2, width, channels), BF16),
        ((2, 2, width, group), BF16),
        *[(tuple(table.shape), table.dtype) for table in constants],
        ((2 * shards, both, width), BF16),
        ((2 * shards, both, width), BF16),
        ((shards, 2, both, width), BF16),
        ((shards, 2, both, width), BF16),
        ((shards, 2, both, width), BF16),
        ((shards, 2, both, width), BF16),
        ((2 * shards, OWN, width), BF16),
        ((2 * shards, OWN, width), BF16),
        ((2 * shards * both, width), F32),
        ((both * shards + both, 4 * width), BF16),
        ((both * shards + both, 4 * width), BF16),
        ((both * shards + both, 4 * width), F32),
        ((2, shards * both, width), F32),
        ((2, shards * both, width), F32),
        ((OWN * shards + extra, 4 * width), BF16),
        ((OWN * shards + extra, 4 * width), BF16),
        ((OWN * shards + extra, 4 * width), F32),
        ((2, shards * OWN, width), F32),
        ((width, channels), BF16),
        ((2, 2, width, group), BF16),
    ]
    return pl.pallas_call(
        functools.partial(kernel, shards),
        out_shape=(
            jax.ShapeDtypeStruct((width, channels), BF16),
            jax.ShapeDtypeStruct((2, 2, width, group), BF16),
        ),
        in_specs=[pl.BlockSpec(memory_space=pl.ANY)] * 9,
        out_specs=[pl.BlockSpec(memory_space=pl.ANY)] * 2,
        scratch_shapes=[pltpu.VMEM(shape, dtype) for shape, dtype in scratch]
        + [
            pltpu.SemaphoreType.DMA((9,)),
            pltpu.SemaphoreType.DMA((4,)),
            pltpu.SemaphoreType.DMA((4,)),
            pltpu.SemaphoreType.DMA((2,)),
        ],
        compiler_params=pltpu.CompilerParams(
            collective_id=0, has_side_effects=True, vmem_limit_bytes=48 << 20
        ),
        name="hyena_backward",
    )(inputs, cotangent, filter_spec, *constants)


def solution(mesh):
    return jax.shard_map(
        local,
        mesh=mesh,
        in_specs=(P(("seq", "chan"), None), P(("seq", "chan"), None), P(None, "seq", None, "chan")),
        out_specs=(P(("seq", "chan"), None), P(None, "seq", None, "chan")),
        check_vma=False,
    )
```

```python
import functools

import jax
import jax.numpy as jnp
import ml_dtypes
import numpy as np
from jax import lax
from jax.experimental import pallas as pl
from jax.experimental.pallas import tpu as pltpu
from jax.sharding import PartitionSpec as P

MESH = pl.DeviceIdType.MESH
OWN = 8
LANES = 128
COLUMN = 16
F32 = jnp.float32
BF16 = jnp.bfloat16


def split(table):
    high = table.astype(ml_dtypes.bfloat16)
    low = (table - high.astype(np.float64)).astype(ml_dtypes.bfloat16)
    return high, low


def angles(left, right, modulus):
    return 2.0 * np.pi * (np.outer(left, right) % modulus) / modulus


@functools.cache
def tables(shards, width):
    classes, offsets = 2 * shards, 2 * width
    points = classes * offsets
    c = np.arange(shards)
    p = np.arange(shards)
    j = np.arange(offsets)
    r = np.arange(width)
    turn = angles(c, p, classes)
    first = np.concatenate([np.cos(turn), -np.sin(turn)])
    first[shards] = np.cos(np.pi * p)
    last = np.concatenate([2.0 * np.cos(turn.T), -2.0 * np.sin(turn.T)], axis=1)
    last[:, 0] = 1.0
    last[:, shards] = np.cos(np.pi * p)
    twist = angles(np.arange(shards + 1), j, points)
    twist_cos, twist_sin = np.cos(twist), -np.sin(twist)
    low, up = angles(j, r, offsets), angles(j, r + 1, offsets)
    inner = np.block(
        [
            [np.cos(low), -np.sin(low), np.cos(up), -np.sin(up)],
            [np.sin(low), np.cos(low), -np.sin(up), -np.cos(up)],
        ]
    )
    edge = np.stack([twist_cos[shards], twist_sin[shards]] + [np.zeros(offsets)] * 6)
    first_high, first_low = split(first)
    last_high, last_low = split(last)
    inner_high, inner_low = split(inner)
    return (
        np.concatenate([first_high, first_low], axis=1),
        np.concatenate([last_high, last_low], axis=0),
        np.stack([inner_high, inner_low]),
        np.stack([inner_high.T, inner_low.T]),
        np.stack([twist_cos[:shards], twist_sin[:shards]]).astype(np.float32),
        edge.astype(np.float32),
    )


def halves(value):
    high = value.astype(BF16)
    return high, (value - high.astype(F32)).astype(BF16)


def dot(left, right):
    return jnp.dot(left, right, preferred_element_type=F32)


def dot3(left_high, left_low, right_ref):
    return (
        dot(left_high, right_ref[0]) + dot(left_high, right_ref[1]) + dot(left_low, right_ref[0])
    )


def kernel(
    shards,
    x_hbm,
    ct_hbm,
    f_hbm,
    first_hbm,
    last_hbm,
    inner_hbm,
    outer_hbm,
    twist_hbm,
    edge_hbm,
    gi_hbm,
    gf_hbm,
    x_v,
    f_v,
    first,
    last,
    inner,
    outer,
    twist,
    edge,
    x_out,
    x_got,
    f_out,
    f_got,
    g_out,
    g_got,
    y_out,
    y_got,
    wide,
    z_high,
    z_low,
    spec,
    f_wide,
    g_wide,
    w_high,
    w_low,
    back,
    y_wide,
    gi_v,
    gf_v,
    load_sem,
    send_sem,
    recv_sem,
    y_sem,
    store_sem,
    plane_sem,
):
    width = LANES
    all_devices = 2 * shards
    points = 4 * shards * width
    both = 2 * OWN
    columns = shards // COLUMN
    planes = 2 * columns
    s, h = lax.axis_index("seq"), lax.axis_index("chan")
    own = h * shards + s
    spot, column = lax.rem(s, COLUMN), lax.div(s, COLUMN)
    place = 2 * column + h

    loads = [
        pltpu.make_async_copy(source, target, load_sem.at[at])
        for at, (source, target) in enumerate(
            (
                (x_hbm, x_v.at[0]),
                (ct_hbm, x_v.at[1]),
                (f_hbm, f_v),
                (first_hbm, first),
                (last_hbm, last),
                (inner_hbm, inner),
                (outer_hbm, outer),
                (twist_hbm, twist),
                (edge_hbm, edge),
            )
        )
    ]
    for load in loads:
        load.start()

    barrier = pltpu.get_barrier_semaphore()

    def in_column(k):
        return column * COLUMN + lax.rem(spot + k, COLUMN), h

    def in_plane(k):
        t = lax.rem(place + k, planes)
        return lax.div(t, 2) * COLUMN + spot, lax.rem(t, 2)

    def signal(semaphore, device):
        pl.semaphore_signal(semaphore, inc=1, device_id=device, device_id_type=MESH)

    for k in range(1, COLUMN):
        signal(barrier, in_column(k))
    for k in range(1, planes):
        signal(barrier, in_plane(k))

    def remote(phase, source, target, device, arrival=None):
        return pltpu.make_async_remote_copy(
            src_ref=source,
            dst_ref=target,
            send_sem=send_sem.at[phase],
            recv_sem=recv_sem.at[phase] if arrival is None else arrival,
            device_id=device,
            device_id_type=MESH,
        )

    def to_column(phase, out, got, k, first_spot, arrival=None):
        t = lax.rem(place + k, planes)
        peer_h, start = lax.rem(t, 2), lax.div(t, 2) * COLUMN
        base = peer_h * shards + start
        for j in range(first_spot, COLUMN):
            at = lax.rem(spot + j, COLUMN)
            remote(phase, out.at[base + at], got.at[own], (start + at, peer_h), arrival).start()

    def to_row(phase, out, got, k, first_spot):
        start = lax.rem(column + k, columns) * COLUMN
        for j in range(first_spot, COLUMN):
            at = start + lax.rem(spot + j, COLUMN)
            remote(phase, out.at[at], got.at[s], (at, h)).start()

    def rest(count, step):
        def body(k, carry):
            step(k)
            return carry

        lax.fori_loop(1, count, body, 0)

    def whole(phase, out, got, count):
        some = pl.ds(0, count - 1)
        return remote(phase, out.at[some], got.at[some], in_plane(1))

    def turn_x(t):
        at = pl.ds(pl.multiple_of(t * LANES, LANES), LANES)
        parts = [x_v[a, :, at].astype(F32).T.reshape(LANES // OWN, OWN, width) for a in range(2)]
        x_out[pl.ds(t * (LANES // OWN), LANES // OWN)] = jnp.concatenate(parts, axis=1).astype(BF16)

    def turn_f(t):
        at = pl.ds(pl.multiple_of(t * LANES, LANES), LANES)
        for g in range(2):
            parts = [
                f_v[part, g, :, at].astype(F32).T.reshape(LANES // OWN, OWN, width)
                for part in range(2)
            ]
            f_out[pl.ds(t * (LANES // OWN), LANES // OWN), g] = jnp.concatenate(
                parts, axis=1
            ).astype(BF16)

    loads[0].wait()
    loads[1].wait()
    turn_x(h * columns + column)
    loads[2].wait()
    turn_f(column)
    rest(planes, lambda k: turn_x(lax.rem(h * columns + column + k, planes)))
    pl.semaphore_wait(barrier, COLUMN - 1 + planes - 1)
    for k in range(1, planes):
        signal(plane_sem, in_plane(k))
    to_column(0, x_out, x_got, 0, 1)
    to_row(1, f_out, f_got, 0, 1)
    rest(columns, lambda k: turn_f(lax.rem(column + k, columns)))
    x_got[own] = x_out[own]
    f_got[s] = f_out[s]
    pl.semaphore_wait(plane_sem, planes - 1)
    rest(planes, lambda k: to_column(0, x_out, x_got, k, 0))
    rest(columns, lambda k: to_row(1, f_out, f_got, k, 0))
    for load in loads[3:]:
        load.wait()

    whole(0, x_out, x_got, all_devices).wait_recv()

    def widen_x(t, carry):
        rows = pl.ds(pl.multiple_of(t * 16 * both, 16 * both), 16 * both)
        wide[rows] = x_got[pl.ds(t * 16, 16)].astype(F32).reshape(16 * both, width)
        return carry

    lax.fori_loop(0, all_devices // 16, widen_x, 0)

    def forward_first(q, carry):
        x = jnp.concatenate(
            [wide[pl.ds(a * shards * both + q, shards, stride=both), :] for a in range(2)], axis=1
        ).astype(BF16)
        y = dot(first[...], jnp.concatenate([x, x], axis=0))
        real, imag = y[:shards], y[shards:]
        alone = imag[0:1]
        zero_row = lax.broadcasted_iota(jnp.int32, imag.shape, 0) == 0
        imag = jnp.where(zero_row, 0.0, imag)
        z = jnp.concatenate(
            [real * twist[0] - imag * twist[1], real * twist[1] + imag * twist[0]], axis=1
        )
        rows = pl.ds(pl.multiple_of(q * shards, shards), shards)
        high, low = halves(z)
        z_high[rows] = high
        z_low[rows] = low
        spec[pl.ds(both * shards + q, 1), :] = jnp.concatenate(
            [alone * edge[0:1], alone * edge[1:2]], axis=1
        )
        return carry

    lax.fori_loop(0, both, forward_first, 0)
    tail = pl.ds(both * shards, both)
    high, low = halves(spec[tail])
    z_high[tail] = high
    z_low[tail] = low

    rows_forward = z_high.shape[0]
    step_forward = rows_forward // 3 if rows_forward % 48 == 0 else rows_forward

    def forward_second(t, carry):
        rows = pl.ds(pl.multiple_of(t * step_forward, 16), step_forward)
        spec[rows] = dot3(z_high[rows], z_low[rows], inner)
        return carry

    lax.fori_loop(0, rows_forward // step_forward, forward_second, 0)

    for q in range(both):
        zero, extra = pl.ds(q * shards, 1), pl.ds(both * shards + q, 1)
        kept = spec[zero, 2 * width : 3 * width]
        spec[zero, 2 * width :] = spec[extra, : 2 * width]
        spec[extra, 2 * width : 3 * width] = kept

    corner = (lax.broadcasted_iota(jnp.int32, (shards, width), 0) == 0) & (
        lax.broadcasted_iota(jnp.int32, (shards, width), 1) == 0
    )

    def spectrum(q, g):
        rows = pl.ds(pl.multiple_of(q * shards, shards), shards)
        at = 2 * width * g
        return spec[rows, at : at + width], spec[rows, at + width : at + 2 * width]

    def top(q):
        return spec[pl.ds(both * shards + q, 1), 3 * width - 1 : 3 * width]

    for ch in range(OWN):
        for g in range(2):
            (ur, ui), (vr, vi) = spectrum(ch, g), spectrum(OWN + ch, g)
            real = (ur * vr + ui * vi) * (2.0 / points)
            imag = (ur * vi - ui * vr) * (2.0 / points)
            if g == 0:
                real = jnp.where(corner, 0.5 * real, real)
                imag = jnp.where(corner, top(ch) * top(OWN + ch) * (1.0 / points), imag)
            g_wide[g, pl.ds(ch, shards, stride=both), :] = real
            g_wide[g, pl.ds(OWN + ch, shards, stride=both), :] = imag

    def narrow_g(t, carry):
        rows = pl.ds(pl.multiple_of(t * 16 * both, 16 * both), 16 * both)
        for g in range(2):
            g_out[pl.ds(t * 16, 16), g] = g_wide[g, rows].reshape(16, both, width).astype(BF16)
        return carry

    lax.fori_loop(0, shards // 16, narrow_g, 0)
    g_got[s] = g_out[s]
    rest(columns, lambda k: to_row(2, g_out, g_got, k, 0))
    to_row(2, g_out, g_got, 0, 1)

    whole(1, f_out, f_got, shards).wait_recv()

    def widen_f(t, carry):
        rows = pl.ds(pl.multiple_of(t * 16 * both, 16 * both), 16 * both)
        for g in range(2):
            f_wide[g, rows] = f_got[pl.ds(t * 16, 16), g].astype(F32).reshape(16 * both, width)
        return carry

    lax.fori_loop(0, shards // 16, widen_f, 0)

    row_at = lax.broadcasted_iota(jnp.int32, (shards, width), 0)
    lane_at = lax.broadcasted_iota(jnp.int32, (shards, width), 1)
    lane_one = lax.broadcasted_iota(jnp.int32, (1, width), 1)
    extra_rows = w_high.shape[0] - OWN * shards
    back[pl.ds(OWN * shards, extra_rows)] = jnp.zeros((extra_rows, 4 * width), F32)
    for ch in range(OWN):
        fields = []
        for g in range(2):
            vr, vi = spectrum(OWN + ch, g)
            fr = f_wide[g, pl.ds(ch, shards, stride=both), :]
            fi = f_wide[g, pl.ds(OWN + ch, shards, stride=both), :]
            if g == 0:
                above = top(OWN + ch) * fi[0:1, 0:1]
                fi = jnp.where(corner, 0.0, fi)
            fields.append((fr * vr + fi * vi, fr * vi - fi * vr))
        (ar, ai), (br, bi) = fields
        back[pl.ds(OWN * shards + ch, 1), : 2 * width] = 2.0 * jnp.concatenate(
            [br[0:1], bi[0:1]], axis=1
        )
        twice = (row_at == 0) & (lane_at > 0)
        ar = jnp.where(twice, 2.0 * ar, ar)
        ai = jnp.where(twice, 2.0 * ai, jnp.where(corner, 0.0, ai))
        br = jnp.where(row_at == 0, jnp.where(lane_one == width - 1, above, 0.0), br)
        bi = jnp.where(row_at == 0, 0.0, bi)
        high, low = halves(jnp.concatenate([ar, ai, br, bi], axis=1))
        rows = pl.ds(ch * shards, shards)
        w_high[rows] = high
        w_low[rows] = low
    tail_back = pl.ds(OWN * shards, extra_rows)
    high, low = halves(back[tail_back])
    w_high[tail_back] = high
    w_low[tail_back] = low

    rows_back = w_high.shape[0]
    step_back = rows_back // 3 if rows_back % 48 == 0 else rows_back

    def inverse_first(t, carry):
        rows = pl.ds(pl.multiple_of(t * step_back, 16), step_back)
        back[rows] = dot3(w_high[rows], w_low[rows], outer)
        return carry

    lax.fori_loop(0, rows_back // step_back, inverse_first, 0)

    for ch in range(OWN):
        rows = pl.ds(ch * shards, shards)
        hr, hi = back[rows, : 2 * width], back[rows, 2 * width :]
        extra = pl.ds(OWN * shards + ch, 1)
        er, ei = back[extra, : 2 * width], back[extra, 2 * width :]
        kr = hr * twist[0] + hi * twist[1]
        ki = hi * twist[0] - hr * twist[1]
        zero_row = lax.broadcasted_iota(jnp.int32, ki.shape, 0) == 0
        ki = jnp.where(zero_row, er * edge[0:1] + ei * edge[1:2], ki)
        high, low = halves(jnp.concatenate([kr, ki], axis=0))
        main = dot(last[...], high)
        y = main[:shards] + main[shards:] + dot(last[pl.ds(0, shards)], low)
        y = y * (1.0 / points)
        for a in range(2):
            y_wide[a, pl.ds(ch, shards, stride=OWN), :] = y[:, a * width : (a + 1) * width]

    def narrow_y(t, carry):
        rows = pl.ds(pl.multiple_of(t * 16 * OWN, 16 * OWN), 16 * OWN)
        for a in range(2):
            y_out[pl.ds(a * shards + t * 16, 16)] = (
                y_wide[a, rows].reshape(16, OWN, width).astype(BF16)
            )
        return carry

    lax.fori_loop(0, shards // 16, narrow_y, 0)
    y_got[own] = y_out[own]
    mine = h * columns + column
    rest(planes, lambda k: to_column(3, y_out, y_got, k, 0, y_sem.at[mine]))
    to_column(3, y_out, y_got, 0, 1, y_sem.at[mine])

    whole(2, g_out, g_got, shards).wait_recv()

    def turn_g(t, carry):
        at = pl.ds(pl.multiple_of(t * LANES, LANES), LANES)
        for g in range(2):
            block = g_got[pl.ds(t * (LANES // OWN), LANES // OWN), g].astype(F32)
            for part in range(2):
                rows = block[:, part * OWN : (part + 1) * OWN].reshape(LANES, width)
                gf_v[part, g, :, at] = rows.T.astype(BF16)
        return carry

    lax.fori_loop(0, shards * OWN // LANES, turn_g, 0)

    store_gf = pltpu.make_async_copy(gf_v, gf_hbm, store_sem.at[0])
    store_gf.start()

    def turn_y(k, missing):
        t = lax.rem(place - k + planes, planes)
        t = lax.rem(t, 2) * columns + lax.div(t, 2)
        first_row = t * COLUMN
        some = pl.ds(first_row, COLUMN - missing)
        remote(3, y_out.at[some], y_got.at[some], in_plane(1), y_sem.at[t]).wait_recv()
        at = pl.ds(pl.multiple_of(t * LANES, LANES), LANES)
        rows = y_got[pl.ds(first_row, COLUMN)].astype(F32).reshape(LANES, width)
        gi_v[:, at] = rows.T.astype(BF16)
        pltpu.make_async_copy(gi_v.at[:, at], gi_hbm.at[:, at], store_sem.at[1]).start()

    rest(planes, lambda k: turn_y(k, 0))
    turn_y(0, 1)

    whole(0, x_out, x_got, all_devices).wait_send()
    whole(1, f_out, f_got, shards).wait_send()
    whole(2, g_out, g_got, shards).wait_send()
    whole(3, y_out, y_got, all_devices).wait_send()
    store_gf.wait()
    pltpu.make_async_copy(gi_v, gi_hbm, store_sem.at[1]).wait()


def local(inputs, cotangent, filter_spec):
    width, channels = inputs.shape
    shards = lax.axis_size("seq")
    group = channels // 2
    both = 2 * OWN
    constants = [jnp.asarray(table) for table in tables(shards, width)]
    extra = 32
    scratch = [
        ((2, width, channels), BF16),
        ((2, 2, width, group), BF16),
        *[(tuple(table.shape), table.dtype) for table in constants],
        ((2 * shards, both, width), BF16),
        ((2 * shards, both, width), BF16),
        ((shards, 2, both, width), BF16),
        ((shards, 2, both, width), BF16),
        ((shards, 2, both, width), BF16),
        ((shards, 2, both, width), BF16),
        ((2 * shards, OWN, width), BF16),
        ((2 * shards, OWN, width), BF16),
        ((2 * shards * both, width), F32),
        ((both * shards + both, 4 * width), BF16),
        ((both * shards + both, 4 * width), BF16),
        ((both * shards + both, 4 * width), F32),
        ((2, shards * both, width), F32),
        ((2, shards * both, width), F32),
        ((OWN * shards + extra, 4 * width), BF16),
        ((OWN * shards + extra, 4 * width), BF16),
        ((OWN * shards + extra, 4 * width), F32),
        ((2, shards * OWN, width), F32),
        ((width, channels), BF16),
        ((2, 2, width, group), BF16),
    ]
    return pl.pallas_call(
        functools.partial(kernel, shards),
        out_shape=(
            jax.ShapeDtypeStruct((width, channels), BF16),
            jax.ShapeDtypeStruct((2, 2, width, group), BF16),
        ),
        in_specs=[pl.BlockSpec(memory_space=pl.ANY)] * 9,
        out_specs=[pl.BlockSpec(memory_space=pl.ANY)] * 2,
        scratch_shapes=[pltpu.VMEM(shape, dtype) for shape, dtype in scratch]
        + [
            pltpu.SemaphoreType.DMA((9,)),
            pltpu.SemaphoreType.DMA((4,)),
            pltpu.SemaphoreType.DMA((3,)),
            pltpu.SemaphoreType.DMA((2 * shards // COLUMN,)),
            pltpu.SemaphoreType.DMA((2,)),
            pltpu.SemaphoreType.REGULAR,
        ],
        compiler_params=pltpu.CompilerParams(
            collective_id=0, has_side_effects=True, vmem_limit_bytes=60 << 20
        ),
        name="hyena_backward",
    )(inputs, cotangent, filter_spec, *constants)


def solution(mesh):
    return jax.shard_map(
        local,
        mesh=mesh,
        in_specs=(P(("seq", "chan"), None), P(("seq", "chan"), None), P(None, "seq", None, "chan")),
        out_specs=(P(("seq", "chan"), None), P(None, "seq", None, "chan")),
        check_vma=False,
    )
```

```python
import functools

import jax
import jax.numpy as jnp
import ml_dtypes
import numpy as np
from jax import lax
from jax.experimental import pallas as pl
from jax.experimental.pallas import tpu as pltpu
from jax.sharding import PartitionSpec as P

MESH = pl.DeviceIdType.MESH
OWN = 8
LANES = 128
COLUMN = 16
F32 = jnp.float32
BF16 = jnp.bfloat16


def split(table):
    high = table.astype(ml_dtypes.bfloat16)
    low = (table - high.astype(np.float64)).astype(ml_dtypes.bfloat16)
    return high, low


def angles(left, right, modulus):
    return 2.0 * np.pi * (np.outer(left, right) % modulus) / modulus


@functools.cache
def tables(shards, width):
    classes, offsets = 2 * shards, 2 * width
    points = classes * offsets
    c = np.arange(shards)
    p = np.arange(shards)
    j = np.arange(offsets)
    r = np.arange(width)
    turn = angles(c, p, classes)
    first = np.concatenate([np.cos(turn), -np.sin(turn)])
    first[shards] = np.cos(np.pi * p)
    last = np.concatenate([2.0 * np.cos(turn.T), -2.0 * np.sin(turn.T)], axis=1)
    last[:, 0] = 1.0
    last[:, shards] = np.cos(np.pi * p)
    twist = angles(np.arange(shards + 1), j, points)
    twist_cos, twist_sin = np.cos(twist), -np.sin(twist)
    low, up = angles(j, r, offsets), angles(j, r + 1, offsets)
    inner = np.block(
        [
            [np.cos(low), -np.sin(low), np.cos(up), -np.sin(up)],
            [np.sin(low), np.cos(low), -np.sin(up), -np.cos(up)],
        ]
    )
    edge = np.stack([twist_cos[shards], twist_sin[shards]] + [np.zeros(offsets)] * 6)
    first_high, first_low = split(first)
    last_high, last_low = split(last)
    inner_high, inner_low = split(inner)
    return (
        np.concatenate([first_high, first_low], axis=1),
        np.concatenate([last_high, last_low], axis=0),
        np.stack([inner_high, inner_low]),
        np.stack([inner_high.T, inner_low.T]),
        np.stack([twist_cos[:shards], twist_sin[:shards]]).astype(np.float32),
        edge.astype(np.float32),
    )


def halves(value):
    high = value.astype(BF16)
    return high, (value - high.astype(F32)).astype(BF16)


def dot(left, right):
    return jnp.dot(left, right, preferred_element_type=F32)


def dot3(left_high, left_low, right_ref):
    return (
        dot(left_high, right_ref[0]) + dot(left_high, right_ref[1]) + dot(left_low, right_ref[0])
    )


def kernel(
    shards,
    x_hbm,
    ct_hbm,
    f_hbm,
    first_hbm,
    last_hbm,
    inner_hbm,
    outer_hbm,
    twist_hbm,
    edge_hbm,
    gi_v,
    gf_v,
    x_v,
    f_v,
    first,
    last,
    inner,
    outer,
    twist,
    edge,
    x_out,
    x_got,
    f_out,
    f_got,
    g_out,
    g_got,
    y_out,
    y_got,
    wide,
    z_high,
    z_low,
    spec,
    f_wide,
    g_wide,
    w_high,
    w_low,
    back,
    y_wide,
    load_sem,
    send_sem,
    recv_sem,
    y_sem,
    plane_sem,
):
    width = LANES
    all_devices = 2 * shards
    points = 4 * shards * width
    both = 2 * OWN
    columns = shards // COLUMN
    planes = 2 * columns
    s, h = lax.axis_index("seq"), lax.axis_index("chan")
    own = h * shards + s
    spot, column = lax.rem(s, COLUMN), lax.div(s, COLUMN)
    place = 2 * column + h

    barrier = pltpu.get_barrier_semaphore()

    def in_column(k):
        return column * COLUMN + lax.rem(spot + k, COLUMN), h

    def in_plane(k):
        t = lax.rem(place + k, planes)
        return lax.div(t, 2) * COLUMN + spot, lax.rem(t, 2)

    def signal(semaphore, device):
        pl.semaphore_signal(semaphore, inc=1, device_id=device, device_id_type=MESH)

    for k in range(1, max(COLUMN, planes)):
        far = COLUMN // 2 + (k // 2 if k % 2 else -(k // 2))
        signal(barrier, in_column(far))
        if k < planes:
            far = planes // 2 + (k // 2 if k % 2 else -(k // 2))
            signal(barrier, in_plane(far))

    loads = [
        pltpu.make_async_copy(source, target, load_sem.at[at])
        for at, (source, target) in enumerate(
            (
                (x_hbm, x_v.at[0]),
                (ct_hbm, x_v.at[1]),
                (f_hbm, f_v),
                (first_hbm, first),
                (last_hbm, last),
                (inner_hbm, inner),
                (outer_hbm, outer),
                (twist_hbm, twist),
                (edge_hbm, edge),
            )
        )
    ]
    for load in loads:
        load.start()

    def remote(phase, source, target, device, arrival=None):
        return pltpu.make_async_remote_copy(
            src_ref=source,
            dst_ref=target,
            send_sem=send_sem.at[phase],
            recv_sem=recv_sem.at[phase] if arrival is None else arrival,
            device_id=device,
            device_id_type=MESH,
        )

    def to_column(phase, out, got, k, first_spot, arrival=None):
        t = lax.rem(place + k, planes)
        peer_h, start = lax.rem(t, 2), lax.div(t, 2) * COLUMN
        base = peer_h * shards + start
        for j in range(first_spot, COLUMN):
            at = lax.rem(spot + j, COLUMN)
            remote(phase, out.at[base + at], got.at[own], (start + at, peer_h), arrival).start()

    def to_row(phase, out, got, k, first_spot):
        start = lax.rem(column + k, columns) * COLUMN
        for j in range(first_spot, COLUMN):
            at = start + lax.rem(spot + j, COLUMN)
            remote(phase, out.at[at], got.at[s], (at, h)).start()

    def rest(count, step):
        def body(k, carry):
            step(k)
            return carry

        lax.fori_loop(1, count, body, 0)

    def whole(phase, out, got, count):
        some = pl.ds(0, count - 1)
        return remote(phase, out.at[some], got.at[some], in_plane(1))

    def turn_x(t):
        at = pl.ds(pl.multiple_of(t * LANES, LANES), LANES)
        parts = [x_v[a, :, at].astype(F32).T.reshape(LANES // OWN, OWN, width) for a in range(2)]
        x_out[pl.ds(t * (LANES // OWN), LANES // OWN)] = jnp.concatenate(parts, axis=1).astype(BF16)

    def turn_f(t):
        at = pl.ds(pl.multiple_of(t * LANES, LANES), LANES)
        for g in range(2):
            parts = [
                f_v[part, g, :, at].astype(F32).T.reshape(LANES // OWN, OWN, width)
                for part in range(2)
            ]
            f_out[pl.ds(t * (LANES // OWN), LANES // OWN), g] = jnp.concatenate(
                parts, axis=1
            ).astype(BF16)

    loads[0].wait()
    loads[1].wait()
    turn_x(h * columns + column)
    loads[2].wait()
    turn_f(column)
    rest(planes, lambda k: turn_x(lax.rem(h * columns + column + k, planes)))
    pl.semaphore_wait(barrier, COLUMN - 1 + planes - 1)
    for k in range(1, planes):
        signal(plane_sem, in_plane(k))
    to_column(0, x_out, x_got, 0, 1)
    to_row(1, f_out, f_got, 0, 1)
    rest(columns, lambda k: turn_f(lax.rem(column + k, columns)))
    x_got[own] = x_out[own]
    f_got[s] = f_out[s]
    pl.semaphore_wait(plane_sem, planes - 1)
    rest(planes, lambda k: to_column(0, x_out, x_got, k, 0))
    rest(columns, lambda k: to_row(1, f_out, f_got, k, 0))
    for load in loads[3:]:
        load.wait()

    whole(0, x_out, x_got, all_devices).wait_recv()

    def widen_x(t, carry):
        rows = pl.ds(pl.multiple_of(t * 16 * both, 16 * both), 16 * both)
        wide[rows] = x_got[pl.ds(t * 16, 16)].astype(F32).reshape(16 * both, width)
        return carry

    lax.fori_loop(0, all_devices // 16, widen_x, 0)

    def forward_first(q, carry):
        x = jnp.concatenate(
            [wide[pl.ds(a * shards * both + q, shards, stride=both), :] for a in range(2)], axis=1
        ).astype(BF16)
        y = dot(first[...], jnp.concatenate([x, x], axis=0))
        real, imag = y[:shards], y[shards:]
        alone = imag[0:1]
        zero_row = lax.broadcasted_iota(jnp.int32, imag.shape, 0) == 0
        imag = jnp.where(zero_row, 0.0, imag)
        z = jnp.concatenate(
            [real * twist[0] - imag * twist[1], real * twist[1] + imag * twist[0]], axis=1
        )
        rows = pl.ds(pl.multiple_of(q * shards, shards), shards)
        high, low = halves(z)
        z_high[rows] = high
        z_low[rows] = low
        spec[pl.ds(both * shards + q, 1), :] = jnp.concatenate(
            [alone * edge[0:1], alone * edge[1:2]], axis=1
        )
        return carry

    lax.fori_loop(0, both, forward_first, 0)
    tail = pl.ds(both * shards, both)
    high, low = halves(spec[tail])
    z_high[tail] = high
    z_low[tail] = low

    rows_forward = z_high.shape[0]
    step_forward = rows_forward // 3 if rows_forward % 48 == 0 else rows_forward

    def forward_second(t, carry):
        rows = pl.ds(pl.multiple_of(t * step_forward, 16), step_forward)
        spec[rows] = dot3(z_high[rows], z_low[rows], inner)
        return carry

    lax.fori_loop(0, rows_forward // step_forward, forward_second, 0)

    for q in range(both):
        zero, extra = pl.ds(q * shards, 1), pl.ds(both * shards + q, 1)
        kept = spec[zero, 2 * width : 3 * width]
        spec[zero, 2 * width :] = spec[extra, : 2 * width]
        spec[extra, 2 * width : 3 * width] = kept

    corner = (lax.broadcasted_iota(jnp.int32, (shards, width), 0) == 0) & (
        lax.broadcasted_iota(jnp.int32, (shards, width), 1) == 0
    )

    def spectrum(q, g):
        rows = pl.ds(pl.multiple_of(q * shards, shards), shards)
        at = 2 * width * g
        return spec[rows, at : at + width], spec[rows, at + width : at + 2 * width]

    def top(q):
        return spec[pl.ds(both * shards + q, 1), 3 * width - 1 : 3 * width]

    for ch in range(OWN):
        for g in range(2):
            (ur, ui), (vr, vi) = spectrum(ch, g), spectrum(OWN + ch, g)
            real = (ur * vr + ui * vi) * (2.0 / points)
            imag = (ur * vi - ui * vr) * (2.0 / points)
            if g == 0:
                real = jnp.where(corner, 0.5 * real, real)
                imag = jnp.where(corner, top(ch) * top(OWN + ch) * (1.0 / points), imag)
            g_wide[g, pl.ds(ch, shards, stride=both), :] = real
            g_wide[g, pl.ds(OWN + ch, shards, stride=both), :] = imag

    def narrow_g(t, carry):
        rows = pl.ds(pl.multiple_of(t * 16 * both, 16 * both), 16 * both)
        for g in range(2):
            g_out[pl.ds(t * 16, 16), g] = g_wide[g, rows].reshape(16, both, width).astype(BF16)
        return carry

    lax.fori_loop(0, shards // 16, narrow_g, 0)
    g_got[s] = g_out[s]
    rest(columns, lambda k: to_row(2, g_out, g_got, k, 0))
    to_row(2, g_out, g_got, 0, 1)

    whole(1, f_out, f_got, shards).wait_recv()

    def widen_f(t, carry):
        rows = pl.ds(pl.multiple_of(t * 16 * both, 16 * both), 16 * both)
        for g in range(2):
            f_wide[g, rows] = f_got[pl.ds(t * 16, 16), g].astype(F32).reshape(16 * both, width)
        return carry

    lax.fori_loop(0, shards // 16, widen_f, 0)

    row_at = lax.broadcasted_iota(jnp.int32, (shards, width), 0)
    lane_at = lax.broadcasted_iota(jnp.int32, (shards, width), 1)
    lane_one = lax.broadcasted_iota(jnp.int32, (1, width), 1)
    extra_rows = w_high.shape[0] - OWN * shards
    back[pl.ds(OWN * shards, extra_rows)] = jnp.zeros((extra_rows, 4 * width), F32)
    for ch in range(OWN):
        fields = []
        for g in range(2):
            vr, vi = spectrum(OWN + ch, g)
            fr = f_wide[g, pl.ds(ch, shards, stride=both), :]
            fi = f_wide[g, pl.ds(OWN + ch, shards, stride=both), :]
            if g == 0:
                above = top(OWN + ch) * fi[0:1, 0:1]
                fi = jnp.where(corner, 0.0, fi)
            fields.append((fr * vr + fi * vi, fr * vi - fi * vr))
        (ar, ai), (br, bi) = fields
        back[pl.ds(OWN * shards + ch, 1), : 2 * width] = 2.0 * jnp.concatenate(
            [br[0:1], bi[0:1]], axis=1
        )
        twice = (row_at == 0) & (lane_at > 0)
        ar = jnp.where(twice, 2.0 * ar, ar)
        ai = jnp.where(twice, 2.0 * ai, jnp.where(corner, 0.0, ai))
        br = jnp.where(row_at == 0, jnp.where(lane_one == width - 1, above, 0.0), br)
        bi = jnp.where(row_at == 0, 0.0, bi)
        high, low = halves(jnp.concatenate([ar, ai, br, bi], axis=1))
        rows = pl.ds(ch * shards, shards)
        w_high[rows] = high
        w_low[rows] = low
    tail_back = pl.ds(OWN * shards, extra_rows)
    high, low = halves(back[tail_back])
    w_high[tail_back] = high
    w_low[tail_back] = low

    rows_back = w_high.shape[0]
    step_back = rows_back // 3 if rows_back % 48 == 0 else rows_back

    def inverse_first(t, carry):
        rows = pl.ds(pl.multiple_of(t * step_back, 16), step_back)
        back[rows] = dot3(w_high[rows], w_low[rows], outer)
        return carry

    lax.fori_loop(0, rows_back // step_back, inverse_first, 0)

    for ch in range(OWN):
        rows = pl.ds(ch * shards, shards)
        hr, hi = back[rows, : 2 * width], back[rows, 2 * width :]
        extra = pl.ds(OWN * shards + ch, 1)
        er, ei = back[extra, : 2 * width], back[extra, 2 * width :]
        kr = hr * twist[0] + hi * twist[1]
        ki = hi * twist[0] - hr * twist[1]
        zero_row = lax.broadcasted_iota(jnp.int32, ki.shape, 0) == 0
        ki = jnp.where(zero_row, er * edge[0:1] + ei * edge[1:2], ki)
        high, low = halves(jnp.concatenate([kr, ki], axis=0))
        main = dot(last[...], high)
        y = main[:shards] + main[shards:] + dot(last[pl.ds(0, shards)], low)
        y = y * (1.0 / points)
        for a in range(2):
            y_wide[a, pl.ds(ch, shards, stride=OWN), :] = y[:, a * width : (a + 1) * width]

    def narrow_y(t, carry):
        rows = pl.ds(pl.multiple_of(t * 16 * OWN, 16 * OWN), 16 * OWN)
        for a in range(2):
            y_out[pl.ds(a * shards + t * 16, 16)] = (
                y_wide[a, rows].reshape(16, OWN, width).astype(BF16)
            )
        return carry

    lax.fori_loop(0, shards // 16, narrow_y, 0)
    y_got[own] = y_out[own]
    mine = h * columns + column
    rest(planes, lambda k: to_column(3, y_out, y_got, k, 0, y_sem.at[mine]))
    to_column(3, y_out, y_got, 0, 1, y_sem.at[mine])

    whole(2, g_out, g_got, shards).wait_recv()

    def turn_g(t, carry):
        at = pl.ds(pl.multiple_of(t * LANES, LANES), LANES)
        for g in range(2):
            block = g_got[pl.ds(t * (LANES // OWN), LANES // OWN), g].astype(F32)
            for part in range(2):
                rows = block[:, part * OWN : (part + 1) * OWN].reshape(LANES, width)
                gf_v[part, g, :, at] = rows.T.astype(BF16)
        return carry

    lax.fori_loop(0, shards * OWN // LANES, turn_g, 0)


    def turn_y(k, missing):
        t = lax.rem(place - k + planes, planes)
        t = lax.rem(t, 2) * columns + lax.div(t, 2)
        first_row = t * COLUMN
        some = pl.ds(first_row, COLUMN - missing)
        remote(3, y_out.at[some], y_got.at[some], in_plane(1), y_sem.at[t]).wait_recv()
        at = pl.ds(pl.multiple_of(t * LANES, LANES), LANES)
        rows = y_got[pl.ds(first_row, COLUMN)].astype(F32).reshape(LANES, width)
        gi_v[:, at] = rows.T.astype(BF16)

    rest(planes, lambda k: turn_y(k, 0))
    turn_y(0, 1)

    whole(0, x_out, x_got, all_devices).wait_send()
    whole(1, f_out, f_got, shards).wait_send()
    whole(2, g_out, g_got, shards).wait_send()
    whole(3, y_out, y_got, all_devices).wait_send()


def local(inputs, cotangent, filter_spec):
    width, channels = inputs.shape
    shards = lax.axis_size("seq")
    group = channels // 2
    both = 2 * OWN
    constants = [jnp.asarray(table) for table in tables(shards, width)]
    extra = 32
    scratch = [
        ((2, width, channels), BF16),
        ((2, 2, width, group), BF16),
        *[(tuple(table.shape), table.dtype) for table in constants],
        ((2 * shards, both, width), BF16),
        ((2 * shards, both, width), BF16),
        ((shards, 2, both, width), BF16),
        ((shards, 2, both, width), BF16),
        ((shards, 2, both, width), BF16),
        ((shards, 2, both, width), BF16),
        ((2 * shards, OWN, width), BF16),
        ((2 * shards, OWN, width), BF16),
        ((2 * shards * both, width), F32),
        ((both * shards + both, 4 * width), BF16),
        ((both * shards + both, 4 * width), BF16),
        ((both * shards + both, 4 * width), F32),
        ((2, shards * both, width), F32),
        ((2, shards * both, width), F32),
        ((OWN * shards + extra, 4 * width), BF16),
        ((OWN * shards + extra, 4 * width), BF16),
        ((OWN * shards + extra, 4 * width), F32),
        ((2, shards * OWN, width), F32),
    ]
    return pl.pallas_call(
        functools.partial(kernel, shards),
        out_shape=(
            pltpu.VMEM((width, channels), BF16),
            pltpu.VMEM((2, 2, width, group), BF16),
        ),
        in_specs=[pl.BlockSpec(memory_space=pl.ANY)] * 9,
        out_specs=[pl.BlockSpec(memory_space=pltpu.VMEM)] * 2,
        scratch_shapes=[pltpu.VMEM(shape, dtype) for shape, dtype in scratch]
        + [
            pltpu.SemaphoreType.DMA((9,)),
            pltpu.SemaphoreType.DMA((4,)),
            pltpu.SemaphoreType.DMA((3,)),
            pltpu.SemaphoreType.DMA((2 * shards // COLUMN,)),
            pltpu.SemaphoreType.REGULAR,
        ],
        compiler_params=pltpu.CompilerParams(
            collective_id=0, has_side_effects=True, vmem_limit_bytes=58 << 20
        ),
        name="hyena_backward",
    )(inputs, cotangent, filter_spec, *constants)


def solution(mesh):
    return jax.shard_map(
        local,
        mesh=mesh,
        in_specs=(P(("seq", "chan"), None), P(("seq", "chan"), None), P(None, "seq", None, "chan")),
        out_specs=(P(("seq", "chan"), None), P(None, "seq", None, "chan")),
        check_vma=False,
    )
```

```python
import functools

import jax
import jax.numpy as jnp
import ml_dtypes
import numpy as np
from jax import lax
from jax.experimental import pallas as pl
from jax.experimental.pallas import tpu as pltpu
from jax.sharding import PartitionSpec as P

MESH = pl.DeviceIdType.MESH
OWN = 8
LANES = 128
COLUMN = 16
F32 = jnp.float32
BF16 = jnp.bfloat16


def split(table):
    high = table.astype(ml_dtypes.bfloat16)
    low = (table - high.astype(np.float64)).astype(ml_dtypes.bfloat16)
    return high, low


def angles(left, right, modulus):
    return 2.0 * np.pi * (np.outer(left, right) % modulus) / modulus


@functools.cache
def tables(shards, width):
    classes, offsets = 2 * shards, 2 * width
    points = classes * offsets
    c = np.arange(shards)
    p = np.arange(shards)
    j = np.arange(offsets)
    r = np.arange(width)
    turn = angles(c, p, classes)
    first = np.concatenate([np.cos(turn), -np.sin(turn)])
    first[shards] = np.cos(np.pi * p)
    last = np.concatenate([2.0 * np.cos(turn.T), -2.0 * np.sin(turn.T)], axis=1)
    last[:, 0] = 1.0
    last[:, shards] = np.cos(np.pi * p)
    twist = angles(np.arange(shards + 1), j, points)
    twist_cos, twist_sin = np.cos(twist), -np.sin(twist)
    low, up = angles(j, r, offsets), angles(j, r + 1, offsets)
    inner = np.block(
        [
            [np.cos(low), -np.sin(low), np.cos(up), -np.sin(up)],
            [np.sin(low), np.cos(low), -np.sin(up), -np.cos(up)],
        ]
    )
    edge = np.stack([twist_cos[shards], twist_sin[shards]] + [np.zeros(offsets)] * 6)
    first_high, first_low = split(first)
    last_high, last_low = split(last)
    inner_high, inner_low = split(inner)
    return (
        np.concatenate([first_high, first_low], axis=1),
        np.concatenate([last_high, last_low], axis=0),
        np.stack([inner_high, inner_low]),
        np.stack([inner_high.T, inner_low.T]),
        np.stack([twist_cos[:shards], twist_sin[:shards]]).astype(np.float32),
        edge.astype(np.float32),
    )


def halves(value):
    high = value.astype(BF16)
    return high, (value - high.astype(F32)).astype(BF16)


def dot(left, right):
    return jnp.dot(left, right, preferred_element_type=F32)


def dot3(left_high, left_low, right_ref):
    return (
        dot(left_high, right_ref[0]) + dot(left_high, right_ref[1]) + dot(left_low, right_ref[0])
    )


def kernel(
    shards,
    x_hbm,
    ct_hbm,
    f_hbm,
    first_hbm,
    last_hbm,
    inner_hbm,
    outer_hbm,
    twist_hbm,
    edge_hbm,
    gi_v,
    gf_v,
    x_v,
    f_v,
    first,
    last,
    inner,
    outer,
    twist,
    edge,
    x_out,
    x_got,
    f_out,
    f_got,
    g_out,
    g_got,
    y_out,
    y_got,
    wide,
    z_high,
    z_low,
    spec,
    f_wide,
    g_wide,
    w_high,
    w_low,
    back,
    y_wide,
    load_sem,
    send_sem,
    recv_sem,
    y_sem,
    plane_sem,
):
    width = LANES
    all_devices = 2 * shards
    points = 4 * shards * width
    both = 2 * OWN
    columns = shards // COLUMN
    planes = 2 * columns
    s, h = lax.axis_index("seq"), lax.axis_index("chan")
    own = h * shards + s
    spot, column = lax.rem(s, COLUMN), lax.div(s, COLUMN)
    place = 2 * column + h

    barrier = pltpu.get_barrier_semaphore()

    def in_column(k):
        return column * COLUMN + lax.rem(spot + k, COLUMN), h

    def in_plane(k):
        t = lax.rem(place + k, planes)
        return lax.div(t, 2) * COLUMN + spot, lax.rem(t, 2)

    def signal(semaphore, device):
        pl.semaphore_signal(semaphore, inc=1, device_id=device, device_id_type=MESH)

    for k in range(1, max(COLUMN, planes)):
        far = COLUMN // 2 + (k // 2 if k % 2 else -(k // 2))
        signal(barrier, in_column(far))
        if k < planes:
            far = planes // 2 + (k // 2 if k % 2 else -(k // 2))
            signal(barrier, in_plane(far))

    loads = [
        pltpu.make_async_copy(source, target, load_sem.at[at])
        for at, (source, target) in enumerate(
            (
                (x_hbm, x_v.at[0]),
                (ct_hbm, x_v.at[1]),
                (f_hbm, f_v),
                (first_hbm, first),
                (last_hbm, last),
                (inner_hbm, inner),
                (outer_hbm, outer),
                (twist_hbm, twist),
                (edge_hbm, edge),
            )
        )
    ]
    for load in loads:
        load.start()

    def remote(phase, source, target, device, arrival=None):
        return pltpu.make_async_remote_copy(
            src_ref=source,
            dst_ref=target,
            send_sem=send_sem.at[phase],
            recv_sem=recv_sem.at[phase] if arrival is None else arrival,
            device_id=device,
            device_id_type=MESH,
        )

    def to_column(phase, out, got, k, first_spot, arrival=None):
        t = lax.rem(place + k, planes)
        peer_h, start = lax.rem(t, 2), lax.div(t, 2) * COLUMN
        base = peer_h * shards + start
        for j in range(first_spot, COLUMN):
            at = lax.rem(spot + j, COLUMN)
            remote(phase, out.at[base + at], got.at[own], (start + at, peer_h), arrival).start()

    def to_row(phase, out, got, k, first_spot):
        start = lax.rem(column + k, columns) * COLUMN
        for j in range(first_spot, COLUMN):
            at = start + lax.rem(spot + j, COLUMN)
            remote(phase, out.at[at], got.at[s], (at, h)).start()

    def rest(count, step):
        def body(k, carry):
            step(k)
            return carry

        lax.fori_loop(1, count, body, 0)

    def whole(phase, out, got, count):
        some = pl.ds(0, count - 1)
        return remote(phase, out.at[some], got.at[some], in_plane(1))

    def turn_x(t):
        at = pl.ds(pl.multiple_of(t * LANES, LANES), LANES)
        parts = [x_v[a, :, at].astype(F32).T.reshape(LANES // OWN, OWN, width) for a in range(2)]
        x_out[pl.ds(t * (LANES // OWN), LANES // OWN)] = jnp.concatenate(parts, axis=1).astype(BF16)

    def turn_f(t):
        at = pl.ds(pl.multiple_of(t * LANES, LANES), LANES)
        for g in range(2):
            parts = [
                f_v[part, g, :, at].astype(F32).T.reshape(LANES // OWN, OWN, width)
                for part in range(2)
            ]
            f_out[pl.ds(t * (LANES // OWN), LANES // OWN), g] = jnp.concatenate(
                parts, axis=1
            ).astype(BF16)

    loads[0].wait()
    loads[1].wait()
    turn_x(h * columns + column)
    loads[2].wait()
    turn_f(column)
    rest(planes, lambda k: turn_x(lax.rem(h * columns + column + k, planes)))
    pl.semaphore_wait(barrier, COLUMN - 1 + planes - 1)
    for k in range(1, planes):
        signal(plane_sem, in_plane(k))
    to_column(0, x_out, x_got, 0, 1)
    to_row(1, f_out, f_got, 0, 1)
    rest(columns, lambda k: turn_f(lax.rem(column + k, columns)))
    x_got[own] = x_out[own]
    f_got[s] = f_out[s]
    pl.semaphore_wait(plane_sem, planes - 1)
    rest(planes, lambda k: to_column(0, x_out, x_got, k, 0))
    rest(columns, lambda k: to_row(1, f_out, f_got, k, 0))
    for load in loads[3:]:
        load.wait()

    whole(0, x_out, x_got, all_devices).wait_recv()

    def widen_x(t, carry):
        rows = pl.ds(pl.multiple_of(t * 16 * both, 16 * both), 16 * both)
        wide[rows] = x_got[pl.ds(t * 16, 16)].astype(F32).reshape(16 * both, width)
        return carry

    lax.fori_loop(0, all_devices // 16, widen_x, 0)

    def forward_first(q, carry):
        x = jnp.concatenate(
            [wide[pl.ds(a * shards * both + q, shards, stride=both), :] for a in range(2)], axis=1
        ).astype(BF16)
        y = dot(first[...], jnp.concatenate([x, x], axis=0))
        real, imag = y[:shards], y[shards:]
        alone = imag[0:1]
        zero_row = lax.broadcasted_iota(jnp.int32, imag.shape, 0) == 0
        imag = jnp.where(zero_row, 0.0, imag)
        z = jnp.concatenate(
            [real * twist[0] - imag * twist[1], real * twist[1] + imag * twist[0]], axis=1
        )
        rows = pl.ds(pl.multiple_of(q * shards, shards), shards)
        high, low = halves(z)
        z_high[rows] = high
        z_low[rows] = low
        spec[pl.ds(both * shards + q, 1), :] = jnp.concatenate(
            [alone * edge[0:1], alone * edge[1:2]], axis=1
        )
        return carry

    lax.fori_loop(0, both, forward_first, 0)
    tail = pl.ds(both * shards, both)
    high, low = halves(spec[tail])
    z_high[tail] = high
    z_low[tail] = low

    rows_forward = z_high.shape[0]
    step_forward = rows_forward // 3 if rows_forward % 48 == 0 else rows_forward

    def forward_second(t, carry):
        rows = pl.ds(pl.multiple_of(t * step_forward, 16), step_forward)
        spec[rows] = dot3(z_high[rows], z_low[rows], inner)
        return carry

    lax.fori_loop(0, rows_forward // step_forward, forward_second, 0)

    for q in range(both):
        zero, extra = pl.ds(q * shards, 1), pl.ds(both * shards + q, 1)
        kept = spec[zero, 2 * width : 3 * width]
        spec[zero, 2 * width :] = spec[extra, : 2 * width]
        spec[extra, 2 * width : 3 * width] = kept

    corner = (lax.broadcasted_iota(jnp.int32, (shards, width), 0) == 0) & (
        lax.broadcasted_iota(jnp.int32, (shards, width), 1) == 0
    )

    def spectrum(q, g):
        rows = pl.ds(pl.multiple_of(q * shards, shards), shards)
        at = 2 * width * g
        return spec[rows, at : at + width], spec[rows, at + width : at + 2 * width]

    def top(q):
        return spec[pl.ds(both * shards + q, 1), 3 * width - 1 : 3 * width]

    for ch in range(OWN):
        for g in range(2):
            (ur, ui), (vr, vi) = spectrum(ch, g), spectrum(OWN + ch, g)
            real = (ur * vr + ui * vi) * (2.0 / points)
            imag = (ur * vi - ui * vr) * (2.0 / points)
            if g == 0:
                real = jnp.where(corner, 0.5 * real, real)
                imag = jnp.where(corner, top(ch) * top(OWN + ch) * (1.0 / points), imag)
            g_wide[g, pl.ds(ch, shards, stride=both), :] = real
            g_wide[g, pl.ds(OWN + ch, shards, stride=both), :] = imag

    def narrow_g(t, carry):
        rows = pl.ds(pl.multiple_of(t * 16 * both, 16 * both), 16 * both)
        for g in range(2):
            g_out[pl.ds(t * 16, 16), g] = g_wide[g, rows].reshape(16, both, width).astype(BF16)
        return carry

    lax.fori_loop(0, shards // 16, narrow_g, 0)
    g_got[s] = g_out[s]
    rest(columns, lambda k: to_row(2, g_out, g_got, k, 0))
    to_row(2, g_out, g_got, 0, 1)

    whole(1, f_out, f_got, shards).wait_recv()

    def widen_f(t, carry):
        rows = pl.ds(pl.multiple_of(t * 16 * both, 16 * both), 16 * both)
        for g in range(2):
            f_wide[g, rows] = f_got[pl.ds(t * 16, 16), g].astype(F32).reshape(16 * both, width)
        return carry

    lax.fori_loop(0, shards // 16, widen_f, 0)

    row_at = lax.broadcasted_iota(jnp.int32, (shards, width), 0)
    lane_at = lax.broadcasted_iota(jnp.int32, (shards, width), 1)
    lane_one = lax.broadcasted_iota(jnp.int32, (1, width), 1)
    extra_rows = w_high.shape[0] - OWN * shards
    back[pl.ds(OWN * shards, extra_rows)] = jnp.zeros((extra_rows, 4 * width), F32)
    for ch in range(OWN):
        fields = []
        for g in range(2):
            vr, vi = spectrum(OWN + ch, g)
            fr = f_wide[g, pl.ds(ch, shards, stride=both), :]
            fi = f_wide[g, pl.ds(OWN + ch, shards, stride=both), :]
            if g == 0:
                above = top(OWN + ch) * fi[0:1, 0:1]
                fi = jnp.where(corner, 0.0, fi)
            fields.append((fr * vr + fi * vi, fr * vi - fi * vr))
        (ar, ai), (br, bi) = fields
        back[pl.ds(OWN * shards + ch, 1), : 2 * width] = 2.0 * jnp.concatenate(
            [br[0:1], bi[0:1]], axis=1
        )
        twice = (row_at == 0) & (lane_at > 0)
        ar = jnp.where(twice, 2.0 * ar, ar)
        ai = jnp.where(twice, 2.0 * ai, jnp.where(corner, 0.0, ai))
        br = jnp.where(row_at == 0, jnp.where(lane_one == width - 1, above, 0.0), br)
        bi = jnp.where(row_at == 0, 0.0, bi)
        high, low = halves(jnp.concatenate([ar, ai, br, bi], axis=1))
        rows = pl.ds(ch * shards, shards)
        w_high[rows] = high
        w_low[rows] = low
    tail_back = pl.ds(OWN * shards, extra_rows)
    high, low = halves(back[tail_back])
    w_high[tail_back] = high
    w_low[tail_back] = low

    rows_back = w_high.shape[0]
    step_back = rows_back // 3 if rows_back % 48 == 0 else rows_back

    def inverse_first(t, carry):
        rows = pl.ds(pl.multiple_of(t * step_back, 16), step_back)
        back[rows] = dot3(w_high[rows], w_low[rows], outer)
        return carry

    lax.fori_loop(0, rows_back // step_back, inverse_first, 0)

    for ch in range(OWN):
        rows = pl.ds(ch * shards, shards)
        hr, hi = back[rows, : 2 * width], back[rows, 2 * width :]
        extra = pl.ds(OWN * shards + ch, 1)
        er, ei = back[extra, : 2 * width], back[extra, 2 * width :]
        kr = hr * twist[0] + hi * twist[1]
        ki = hi * twist[0] - hr * twist[1]
        zero_row = lax.broadcasted_iota(jnp.int32, ki.shape, 0) == 0
        ki = jnp.where(zero_row, er * edge[0:1] + ei * edge[1:2], ki)
        high, low = halves(jnp.concatenate([kr, ki], axis=0))
        main = dot(last[...], high)
        y = main[:shards] + main[shards:] + dot(last[pl.ds(0, shards)], low)
        y = y * (1.0 / points)
        for a in range(2):
            y_wide[a, pl.ds(ch, shards, stride=OWN), :] = y[:, a * width : (a + 1) * width]

    def narrow_y(t, carry):
        rows = pl.ds(pl.multiple_of(t * 16 * OWN, 16 * OWN), 16 * OWN)
        for a in range(2):
            y_out[pl.ds(a * shards + t * 16, 16)] = (
                y_wide[a, rows].reshape(16, OWN, width).astype(BF16)
            )
        return carry

    lax.fori_loop(0, shards // 16, narrow_y, 0)
    y_got[own] = y_out[own]
    mine = h * columns + column
    rest(planes, lambda k: to_column(3, y_out, y_got, k, 0, y_sem.at[mine]))
    to_column(3, y_out, y_got, 0, 1, y_sem.at[mine])

    whole(2, g_out, g_got, shards).wait_recv()

    def turn_g(t, carry):
        at = pl.ds(pl.multiple_of(t * LANES, LANES), LANES)
        for g in range(2):
            block = g_got[pl.ds(t * (LANES // OWN), LANES // OWN), g].astype(F32)
            for part in range(2):
                rows = block[:, part * OWN : (part + 1) * OWN].reshape(LANES, width)
                gf_v[part, g, :, at] = rows.T.astype(BF16)
        return carry

    lax.fori_loop(0, shards * OWN // LANES, turn_g, 0)


    def turn_y(k, missing):
        t = lax.rem(place - k + planes, planes)
        t = lax.rem(t, 2) * columns + lax.div(t, 2)
        first_row = t * COLUMN
        some = pl.ds(first_row, COLUMN - missing)
        remote(3, y_out.at[some], y_got.at[some], in_plane(1), y_sem.at[t]).wait_recv()
        at = pl.ds(pl.multiple_of(t * LANES, LANES), LANES)
        rows = y_got[pl.ds(first_row, COLUMN)].astype(F32).reshape(LANES, width)
        gi_v[:, at] = rows.T.astype(BF16)

    rest(planes, lambda k: turn_y(k, 0))
    turn_y(0, 1)

    whole(0, x_out, x_got, all_devices).wait_send()
    whole(1, f_out, f_got, shards).wait_send()
    whole(2, g_out, g_got, shards).wait_send()
    whole(3, y_out, y_got, all_devices).wait_send()


def place(gi, gf, gi_hbm, gf_hbm, sem):
    first = pltpu.make_async_copy(gf, gf_hbm, sem.at[0])
    second = pltpu.make_async_copy(gi, gi_hbm, sem.at[1])
    first.start()
    second.start()
    first.wait()
    second.wait()


def local(inputs, cotangent, filter_spec):
    width, channels = inputs.shape
    shards = lax.axis_size("seq")
    group = channels // 2
    both = 2 * OWN
    constants = [jnp.asarray(table) for table in tables(shards, width)]
    extra = 32
    scratch = [
        ((2, width, channels), BF16),
        ((2, 2, width, group), BF16),
        *[(tuple(table.shape), table.dtype) for table in constants],
        ((2 * shards, both, width), BF16),
        ((2 * shards, both, width), BF16),
        ((shards, 2, both, width), BF16),
        ((shards, 2, both, width), BF16),
        ((shards, 2, both, width), BF16),
        ((shards, 2, both, width), BF16),
        ((2 * shards, OWN, width), BF16),
        ((2 * shards, OWN, width), BF16),
        ((2 * shards * both, width), F32),
        ((both * shards + both, 4 * width), BF16),
        ((both * shards + both, 4 * width), BF16),
        ((both * shards + both, 4 * width), F32),
        ((2, shards * both, width), F32),
        ((2, shards * both, width), F32),
        ((OWN * shards + extra, 4 * width), BF16),
        ((OWN * shards + extra, 4 * width), BF16),
        ((OWN * shards + extra, 4 * width), F32),
        ((2, shards * OWN, width), F32),
    ]
    gradients = pl.pallas_call(
        functools.partial(kernel, shards),
        out_shape=(
            pltpu.VMEM((width, channels), BF16),
            pltpu.VMEM((2, 2, width, group), BF16),
        ),
        in_specs=[pl.BlockSpec(memory_space=pl.ANY)] * 9,
        out_specs=[pl.BlockSpec(memory_space=pltpu.VMEM)] * 2,
        scratch_shapes=[pltpu.VMEM(shape, dtype) for shape, dtype in scratch]
        + [
            pltpu.SemaphoreType.DMA((9,)),
            pltpu.SemaphoreType.DMA((4,)),
            pltpu.SemaphoreType.DMA((3,)),
            pltpu.SemaphoreType.DMA((2 * shards // COLUMN,)),
            pltpu.SemaphoreType.REGULAR,
        ],
        compiler_params=pltpu.CompilerParams(
            collective_id=0, has_side_effects=True, vmem_limit_bytes=58 << 20
        ),
        name="hyena_backward",
    )(inputs, cotangent, filter_spec, *constants)
    return pl.pallas_call(
        place,
        out_shape=(
            pltpu.HBM((width, channels), BF16),
            pltpu.HBM((2, 2, width, group), BF16),
        ),
        in_specs=[pl.BlockSpec(memory_space=pltpu.VMEM)] * 2,
        out_specs=[pl.BlockSpec(memory_space=pl.ANY)] * 2,
        scratch_shapes=[pltpu.SemaphoreType.DMA((2,))],
        name="place",
    )(*[pltpu.with_memory_space_constraint(g, pltpu.VMEM) for g in gradients])


def solution(mesh):
    return jax.shard_map(
        local,
        mesh=mesh,
        in_specs=(P(("seq", "chan"), None), P(("seq", "chan"), None), P(None, "seq", None, "chan")),
        out_specs=(P(("seq", "chan"), None), P(None, "seq", None, "chan")),
        check_vma=False,
    )
```

```python
import functools

import jax
import jax.numpy as jnp
import ml_dtypes
import numpy as np
from jax import lax
from jax.experimental import pallas as pl
from jax.experimental.pallas import tpu as pltpu
from jax.sharding import PartitionSpec as P

MESH = pl.DeviceIdType.MESH
OWN = 8
LANES = 128
COLUMN = 16
LEADS = (8, 6, 5, 3, 0, 0, 0, 0)
F32 = jnp.float32
BF16 = jnp.bfloat16


def split(table):
    high = table.astype(ml_dtypes.bfloat16)
    low = (table - high.astype(np.float64)).astype(ml_dtypes.bfloat16)
    return high, low


def angles(left, right, modulus):
    return 2.0 * np.pi * (np.outer(left, right) % modulus) / modulus


@functools.cache
def tables(shards, width):
    classes, offsets = 2 * shards, 2 * width
    points = classes * offsets
    c = np.arange(shards)
    p = np.arange(shards)
    j = np.arange(offsets)
    r = np.arange(width)
    turn = angles(c, p, classes)
    first = np.concatenate([np.cos(turn), -np.sin(turn)])
    first[shards] = np.cos(np.pi * p)
    last = np.concatenate([2.0 * np.cos(turn.T), -2.0 * np.sin(turn.T)], axis=1)
    last[:, 0] = 1.0
    last[:, shards] = np.cos(np.pi * p)
    twist = angles(np.arange(shards + 1), j, points)
    twist_cos, twist_sin = np.cos(twist), -np.sin(twist)
    low, up = angles(j, r, offsets), angles(j, r + 1, offsets)
    inner = np.block(
        [
            [np.cos(low), -np.sin(low), np.cos(up), -np.sin(up)],
            [np.sin(low), np.cos(low), -np.sin(up), -np.cos(up)],
        ]
    )
    edge = np.stack([twist_cos[shards], twist_sin[shards]] + [np.zeros(offsets)] * 6)
    first_high, first_low = split(first)
    last_high, last_low = split(last)
    inner_high, inner_low = split(inner)
    return (
        np.concatenate([first_high, first_low], axis=1),
        np.concatenate([last_high, last_low], axis=0),
        np.stack([inner_high, inner_low]),
        np.stack([inner_high.T, inner_low.T]),
        np.stack([twist_cos[:shards], twist_sin[:shards]]).astype(np.float32),
        edge.astype(np.float32),
    )


def halves(value):
    high = value.astype(BF16)
    return high, (value - high.astype(F32)).astype(BF16)


def dot(left, right):
    return jnp.dot(left, right, preferred_element_type=F32)


def dot3(left_high, left_low, right_ref):
    return (
        dot(left_high, right_ref[0]) + dot(left_high, right_ref[1]) + dot(left_low, right_ref[0])
    )


def kernel(
    shards,
    x_hbm,
    ct_hbm,
    f_hbm,
    first_hbm,
    last_hbm,
    inner_hbm,
    outer_hbm,
    twist_hbm,
    edge_hbm,
    gi_v,
    gf_v,
    x_v,
    f_v,
    first,
    last,
    inner,
    outer,
    twist,
    edge,
    x_out,
    x_got,
    f_out,
    f_got,
    g_out,
    g_got,
    y_out,
    y_got,
    wide,
    z_high,
    z_low,
    spec,
    f_wide,
    g_wide,
    w_high,
    w_low,
    back,
    y_wide,
    load_sem,
    send_sem,
    recv_sem,
    y_sem,
    plane_sem,
):
    width = LANES
    all_devices = 2 * shards
    points = 4 * shards * width
    both = 2 * OWN
    columns = shards // COLUMN
    planes = 2 * columns
    s, h = lax.axis_index("seq"), lax.axis_index("chan")
    own = h * shards + s
    spot, column = lax.rem(s, COLUMN), lax.div(s, COLUMN)
    place = 2 * column + h

    barrier = pltpu.get_barrier_semaphore()

    def in_column(k):
        return column * COLUMN + lax.rem(spot + k, COLUMN), h

    def in_plane(k):
        t = lax.rem(place + k, planes)
        return lax.div(t, 2) * COLUMN + spot, lax.rem(t, 2)

    def signal(semaphore, device):
        pl.semaphore_signal(semaphore, inc=1, device_id=device, device_id_type=MESH)

    for k in range(1, max(COLUMN, planes)):
        far = COLUMN // 2 + (k // 2 if k % 2 else -(k // 2))
        signal(barrier, in_column(far))
        if k < planes:
            far = planes // 2 + (k // 2 if k % 2 else -(k // 2))
            signal(barrier, in_plane(far))

    loads = [
        pltpu.make_async_copy(source, target, load_sem.at[at])
        for at, (source, target) in enumerate(
            (
                (x_hbm, x_v.at[0]),
                (ct_hbm, x_v.at[1]),
                (f_hbm, f_v),
                (first_hbm, first),
                (last_hbm, last),
                (inner_hbm, inner),
                (outer_hbm, outer),
                (twist_hbm, twist),
                (edge_hbm, edge),
            )
        )
    ]
    for load in loads:
        load.start()

    def remote(phase, source, target, device, arrival=None):
        return pltpu.make_async_remote_copy(
            src_ref=source,
            dst_ref=target,
            send_sem=send_sem.at[phase],
            recv_sem=recv_sem.at[phase] if arrival is None else arrival,
            device_id=device,
            device_id_type=MESH,
        )

    def to_column(phase, out, got, k, first_spot, arrival=None):
        t = lax.rem(place + k, planes)
        peer_h, start = lax.rem(t, 2), lax.div(t, 2) * COLUMN
        base = peer_h * shards + start
        for j in range(first_spot, COLUMN):
            at = lax.rem(spot + j, COLUMN)
            remote(phase, out.at[base + at], got.at[own], (start + at, peer_h), arrival).start()

    def to_row(phase, out, got, k, first_spot):
        start = lax.rem(column + k, columns) * COLUMN
        for j in range(first_spot, COLUMN):
            at = start + lax.rem(spot + j, COLUMN)
            remote(phase, out.at[at], got.at[s], (at, h)).start()

    def rest(count, step):
        def body(k, carry):
            step(k)
            return carry

        lax.fori_loop(1, count, body, 0)

    def whole(phase, out, got, count):
        some = pl.ds(0, count - 1)
        return remote(phase, out.at[some], got.at[some], in_plane(1))

    def turn_x(t):
        at = pl.ds(pl.multiple_of(t * LANES, LANES), LANES)
        parts = [x_v[a, :, at].astype(F32).T.reshape(LANES // OWN, OWN, width) for a in range(2)]
        x_out[pl.ds(t * (LANES // OWN), LANES // OWN)] = jnp.concatenate(parts, axis=1).astype(BF16)

    def turn_f(t):
        at = pl.ds(pl.multiple_of(t * LANES, LANES), LANES)
        for g in range(2):
            parts = [
                f_v[part, g, :, at].astype(F32).T.reshape(LANES // OWN, OWN, width)
                for part in range(2)
            ]
            f_out[pl.ds(t * (LANES // OWN), LANES // OWN), g] = jnp.concatenate(
                parts, axis=1
            ).astype(BF16)

    loads[0].wait()
    loads[1].wait()
    turn_x(h * columns + column)
    loads[2].wait()
    turn_f(column)
    rest(planes, lambda k: turn_x(lax.rem(h * columns + column + k, planes)))
    pl.semaphore_wait(barrier, COLUMN - 1 + planes - 1)
    for k in range(1, planes):
        signal(plane_sem, in_plane(k))
    to_column(0, x_out, x_got, 0, 1)
    to_row(1, f_out, f_got, 0, 1)
    rest(columns, lambda k: turn_f(lax.rem(column + k, columns)))
    x_got[own] = x_out[own]
    f_got[s] = f_out[s]
    pl.semaphore_wait(plane_sem, planes - 1)
    rest(planes, lambda k: to_column(0, x_out, x_got, k, 0))
    rest(columns, lambda k: to_row(1, f_out, f_got, k, 0))
    for load in loads[3:]:
        load.wait()

    whole(0, x_out, x_got, all_devices).wait_recv()

    def widen_x(t, carry):
        rows = pl.ds(pl.multiple_of(t * 16 * both, 16 * both), 16 * both)
        wide[rows] = x_got[pl.ds(t * 16, 16)].astype(F32).reshape(16 * both, width)
        return carry

    lax.fori_loop(0, all_devices // 16, widen_x, 0)

    def forward_first(q, carry):
        x = jnp.concatenate(
            [wide[pl.ds(a * shards * both + q, shards, stride=both), :] for a in range(2)], axis=1
        ).astype(BF16)
        y = dot(first[...], jnp.concatenate([x, x], axis=0))
        real, imag = y[:shards], y[shards:]
        alone = imag[0:1]
        zero_row = lax.broadcasted_iota(jnp.int32, imag.shape, 0) == 0
        imag = jnp.where(zero_row, 0.0, imag)
        z = jnp.concatenate(
            [real * twist[0] - imag * twist[1], real * twist[1] + imag * twist[0]], axis=1
        )
        rows = pl.ds(pl.multiple_of(q * shards, shards), shards)
        high, low = halves(z)
        z_high[rows] = high
        z_low[rows] = low
        spec[pl.ds(both * shards + q, 1), :] = jnp.concatenate(
            [alone * edge[0:1], alone * edge[1:2]], axis=1
        )
        return carry

    lax.fori_loop(0, both, forward_first, 0)
    tail = pl.ds(both * shards, both)
    high, low = halves(spec[tail])
    z_high[tail] = high
    z_low[tail] = low

    rows_forward = z_high.shape[0]
    step_forward = rows_forward // 3 if rows_forward % 48 == 0 else rows_forward

    def forward_second(t, carry):
        rows = pl.ds(pl.multiple_of(t * step_forward, 16), step_forward)
        spec[rows] = dot3(z_high[rows], z_low[rows], inner)
        return carry

    lax.fori_loop(0, rows_forward // step_forward, forward_second, 0)

    for q in range(both):
        zero, extra = pl.ds(q * shards, 1), pl.ds(both * shards + q, 1)
        kept = spec[zero, 2 * width : 3 * width]
        spec[zero, 2 * width :] = spec[extra, : 2 * width]
        spec[extra, 2 * width : 3 * width] = kept

    corner = (lax.broadcasted_iota(jnp.int32, (shards, width), 0) == 0) & (
        lax.broadcasted_iota(jnp.int32, (shards, width), 1) == 0
    )

    def spectrum(q, g):
        rows = pl.ds(pl.multiple_of(q * shards, shards), shards)
        at = 2 * width * g
        return spec[rows, at : at + width], spec[rows, at + width : at + 2 * width]

    def top(q):
        return spec[pl.ds(both * shards + q, 1), 3 * width - 1 : 3 * width]

    for ch in range(OWN):
        for g in range(2):
            (ur, ui), (vr, vi) = spectrum(ch, g), spectrum(OWN + ch, g)
            real = (ur * vr + ui * vi) * (2.0 / points)
            imag = (ur * vi - ui * vr) * (2.0 / points)
            if g == 0:
                real = jnp.where(corner, 0.5 * real, real)
                imag = jnp.where(corner, top(ch) * top(OWN + ch) * (1.0 / points), imag)
            g_wide[g, pl.ds(ch, shards, stride=both), :] = real
            g_wide[g, pl.ds(OWN + ch, shards, stride=both), :] = imag

    def narrow_g(t, carry):
        rows = pl.ds(pl.multiple_of(t * 16 * both, 16 * both), 16 * both)
        for g in range(2):
            g_out[pl.ds(t * 16, 16), g] = g_wide[g, rows].reshape(16, both, width).astype(BF16)
        return carry

    lax.fori_loop(0, shards // 16, narrow_g, 0)
    g_got[s] = g_out[s]
    rest(columns, lambda k: to_row(2, g_out, g_got, k, 0))
    to_row(2, g_out, g_got, 0, 1)

    whole(1, f_out, f_got, shards).wait_recv()

    def widen_f(t, carry):
        rows = pl.ds(pl.multiple_of(t * 16 * both, 16 * both), 16 * both)
        for g in range(2):
            f_wide[g, rows] = f_got[pl.ds(t * 16, 16), g].astype(F32).reshape(16 * both, width)
        return carry

    lax.fori_loop(0, shards // 16, widen_f, 0)

    row_at = lax.broadcasted_iota(jnp.int32, (shards, width), 0)
    lane_at = lax.broadcasted_iota(jnp.int32, (shards, width), 1)
    lane_one = lax.broadcasted_iota(jnp.int32, (1, width), 1)
    extra_rows = w_high.shape[0] - OWN * shards
    back[pl.ds(OWN * shards, extra_rows)] = jnp.zeros((extra_rows, 4 * width), F32)
    for ch in range(OWN):
        fields = []
        for g in range(2):
            vr, vi = spectrum(OWN + ch, g)
            fr = f_wide[g, pl.ds(ch, shards, stride=both), :]
            fi = f_wide[g, pl.ds(OWN + ch, shards, stride=both), :]
            if g == 0:
                above = top(OWN + ch) * fi[0:1, 0:1]
                fi = jnp.where(corner, 0.0, fi)
            fields.append((fr * vr + fi * vi, fr * vi - fi * vr))
        (ar, ai), (br, bi) = fields
        back[pl.ds(OWN * shards + ch, 1), : 2 * width] = 2.0 * jnp.concatenate(
            [br[0:1], bi[0:1]], axis=1
        )
        twice = (row_at == 0) & (lane_at > 0)
        ar = jnp.where(twice, 2.0 * ar, ar)
        ai = jnp.where(twice, 2.0 * ai, jnp.where(corner, 0.0, ai))
        br = jnp.where(row_at == 0, jnp.where(lane_one == width - 1, above, 0.0), br)
        bi = jnp.where(row_at == 0, 0.0, bi)
        high, low = halves(jnp.concatenate([ar, ai, br, bi], axis=1))
        rows = pl.ds(ch * shards, shards)
        w_high[rows] = high
        w_low[rows] = low
    tail_back = pl.ds(OWN * shards, extra_rows)
    high, low = halves(back[tail_back])
    w_high[tail_back] = high
    w_low[tail_back] = low

    rows_back = w_high.shape[0]
    step_back = rows_back // 3 if rows_back % 48 == 0 else rows_back

    def inverse_first(t, carry):
        rows = pl.ds(pl.multiple_of(t * step_back, 16), step_back)
        back[rows] = dot3(w_high[rows], w_low[rows], outer)
        return carry

    lax.fori_loop(0, rows_back // step_back, inverse_first, 0)

    for ch in range(OWN):
        rows = pl.ds(ch * shards, shards)
        hr, hi = back[rows, : 2 * width], back[rows, 2 * width :]
        extra = pl.ds(OWN * shards + ch, 1)
        er, ei = back[extra, : 2 * width], back[extra, 2 * width :]
        kr = hr * twist[0] + hi * twist[1]
        ki = hi * twist[0] - hr * twist[1]
        zero_row = lax.broadcasted_iota(jnp.int32, ki.shape, 0) == 0
        ki = jnp.where(zero_row, er * edge[0:1] + ei * edge[1:2], ki)
        high, low = halves(jnp.concatenate([kr, ki], axis=0))
        main = dot(last[...], high)
        y = main[:shards] + main[shards:] + dot(last[pl.ds(0, shards)], low)
        y = y * (1.0 / points)
        for a in range(2):
            y_wide[a, pl.ds(ch, shards, stride=OWN), :] = y[:, a * width : (a + 1) * width]

    def narrow_y(t, carry):
        rows = pl.ds(pl.multiple_of(t * 16 * OWN, 16 * OWN), 16 * OWN)
        for a in range(2):
            y_out[pl.ds(a * shards + t * 16, 16)] = (
                y_wide[a, rows].reshape(16, OWN, width).astype(BF16)
            )
        return carry

    lax.fori_loop(0, shards // 16, narrow_y, 0)
    y_got[own] = y_out[own]
    mine = h * columns + column

    def y_to(k, at):
        t = lax.rem(place + k, planes)
        peer_h, start = lax.rem(t, 2), lax.div(t, 2) * COLUMN
        remote(
            3, y_out.at[peer_h * shards + start + at], y_got.at[own], (start + at, peer_h), y_sem.at[mine]
        ).start()

    most = max(LEADS)

    def send_y(step, carry):
        for z, lead in enumerate(LEADS):
            m = step - (most - lead)

            @pl.when((m >= 0) & (m < planes))
            def _():
                k = lax.rem(m + 1, planes)
                for core in range(2):
                    at = 2 * z + core

                    @pl.when((k > 0) | (spot != at))
                    def _():
                        y_to(k, at)

        return carry

    lax.fori_loop(0, planes + most, send_y, 0)

    whole(2, g_out, g_got, shards).wait_recv()

    def turn_g(t, carry):
        at = pl.ds(pl.multiple_of(t * LANES, LANES), LANES)
        for g in range(2):
            block = g_got[pl.ds(t * (LANES // OWN), LANES // OWN), g].astype(F32)
            for part in range(2):
                rows = block[:, part * OWN : (part + 1) * OWN].reshape(LANES, width)
                gf_v[part, g, :, at] = rows.T.astype(BF16)
        return carry

    lax.fori_loop(0, shards * OWN // LANES, turn_g, 0)


    def turn_y(k, missing):
        t = lax.rem(place - k + planes, planes)
        t = lax.rem(t, 2) * columns + lax.div(t, 2)
        first_row = t * COLUMN
        some = pl.ds(first_row, COLUMN - missing)
        remote(3, y_out.at[some], y_got.at[some], in_plane(1), y_sem.at[t]).wait_recv()
        at = pl.ds(pl.multiple_of(t * LANES, LANES), LANES)
        rows = y_got[pl.ds(first_row, COLUMN)].astype(F32).reshape(LANES, width)
        gi_v[:, at] = rows.T.astype(BF16)

    rest(planes, lambda k: turn_y(k, 0))
    turn_y(0, 1)

    whole(0, x_out, x_got, all_devices).wait_send()
    whole(1, f_out, f_got, shards).wait_send()
    whole(2, g_out, g_got, shards).wait_send()
    whole(3, y_out, y_got, all_devices).wait_send()


def place(gi, gf, gi_hbm, gf_hbm, sem):
    first = pltpu.make_async_copy(gf, gf_hbm, sem.at[0])
    second = pltpu.make_async_copy(gi, gi_hbm, sem.at[1])
    first.start()
    second.start()
    first.wait()
    second.wait()


def local(inputs, cotangent, filter_spec):
    width, channels = inputs.shape
    shards = lax.axis_size("seq")
    group = channels // 2
    both = 2 * OWN
    constants = [jnp.asarray(table) for table in tables(shards, width)]
    extra = 32
    scratch = [
        ((2, width, channels), BF16),
        ((2, 2, width, group), BF16),
        *[(tuple(table.shape), table.dtype) for table in constants],
        ((2 * shards, both, width), BF16),
        ((2 * shards, both, width), BF16),
        ((shards, 2, both, width), BF16),
        ((shards, 2, both, width), BF16),
        ((shards, 2, both, width), BF16),
        ((shards, 2, both, width), BF16),
        ((2 * shards, OWN, width), BF16),
        ((2 * shards, OWN, width), BF16),
        ((2 * shards * both, width), F32),
        ((both * shards + both, 4 * width), BF16),
        ((both * shards + both, 4 * width), BF16),
        ((both * shards + both, 4 * width), F32),
        ((2, shards * both, width), F32),
        ((2, shards * both, width), F32),
        ((OWN * shards + extra, 4 * width), BF16),
        ((OWN * shards + extra, 4 * width), BF16),
        ((OWN * shards + extra, 4 * width), F32),
        ((2, shards * OWN, width), F32),
    ]
    gradients = pl.pallas_call(
        functools.partial(kernel, shards),
        out_shape=(
            pltpu.VMEM((width, channels), BF16),
            pltpu.VMEM((2, 2, width, group), BF16),
        ),
        in_specs=[pl.BlockSpec(memory_space=pl.ANY)] * 9,
        out_specs=[pl.BlockSpec(memory_space=pltpu.VMEM)] * 2,
        scratch_shapes=[pltpu.VMEM(shape, dtype) for shape, dtype in scratch]
        + [
            pltpu.SemaphoreType.DMA((9,)),
            pltpu.SemaphoreType.DMA((4,)),
            pltpu.SemaphoreType.DMA((3,)),
            pltpu.SemaphoreType.DMA((2 * shards // COLUMN,)),
            pltpu.SemaphoreType.REGULAR,
        ],
        compiler_params=pltpu.CompilerParams(
            collective_id=0, has_side_effects=True, vmem_limit_bytes=58 << 20
        ),
        name="hyena_backward",
    )(inputs, cotangent, filter_spec, *constants)
    return pl.pallas_call(
        place,
        out_shape=(
            pltpu.HBM((width, channels), BF16),
            pltpu.HBM((2, 2, width, group), BF16),
        ),
        in_specs=[pl.BlockSpec(memory_space=pltpu.VMEM)] * 2,
        out_specs=[pl.BlockSpec(memory_space=pl.ANY)] * 2,
        scratch_shapes=[pltpu.SemaphoreType.DMA((2,))],
        name="place",
    )(*[pltpu.with_memory_space_constraint(g, pltpu.VMEM) for g in gradients])


def solution(mesh):
    return jax.shard_map(
        local,
        mesh=mesh,
        in_specs=(P(("seq", "chan"), None), P(("seq", "chan"), None), P(None, "seq", None, "chan")),
        out_specs=(P(("seq", "chan"), None), P(None, "seq", None, "chan")),
        check_vma=False,
    )
```

```python
import functools

import jax
import jax.numpy as jnp
import ml_dtypes
import numpy as np
from jax import lax
from jax.experimental import pallas as pl
from jax.experimental.pallas import tpu as pltpu
from jax.sharding import PartitionSpec as P

MESH = pl.DeviceIdType.MESH
OWN = 8
LANES = 128
COLUMN = 16
LEADS = (8, 6, 5, 3, 0, 0, 0, 0)
F32 = jnp.float32
BF16 = jnp.bfloat16


def split(table):
    high = table.astype(ml_dtypes.bfloat16)
    low = (table - high.astype(np.float64)).astype(ml_dtypes.bfloat16)
    return high, low


def angles(left, right, modulus):
    return 2.0 * np.pi * (np.outer(left, right) % modulus) / modulus


@functools.cache
def tables(shards, width):
    classes, offsets = 2 * shards, 2 * width
    points = classes * offsets
    c = np.arange(shards)
    p = np.arange(shards)
    j = np.arange(offsets)
    r = np.arange(width)
    turn = angles(c, p, classes)
    first = np.concatenate([np.cos(turn), -np.sin(turn)])
    first[shards] = np.cos(np.pi * p)
    last = np.concatenate([2.0 * np.cos(turn.T), -2.0 * np.sin(turn.T)], axis=1)
    last[:, 0] = 1.0
    last[:, shards] = np.cos(np.pi * p)
    twist = angles(np.arange(shards + 1), j, points)
    twist_cos, twist_sin = np.cos(twist), -np.sin(twist)
    low, up = angles(j, r, offsets), angles(j, r + 1, offsets)
    inner = np.block(
        [
            [np.cos(low), -np.sin(low), np.cos(up), -np.sin(up)],
            [np.sin(low), np.cos(low), -np.sin(up), -np.cos(up)],
        ]
    )
    edge = np.stack([twist_cos[shards], twist_sin[shards]] + [np.zeros(offsets)] * 6)
    first_high, first_low = split(first)
    last_high, last_low = split(last)
    inner_high, inner_low = split(inner)
    return (
        np.concatenate([first_high, first_low], axis=1),
        np.concatenate([last_high, last_low], axis=0),
        np.stack([inner_high, inner_low]),
        np.stack([inner_high.T, inner_low.T]),
        np.stack([twist_cos[:shards], twist_sin[:shards]]).astype(np.float32),
        edge.astype(np.float32),
    )


def halves(value):
    high = value.astype(BF16)
    return high, (value - high.astype(F32)).astype(BF16)


def dot(left, right):
    return jnp.dot(left, right, preferred_element_type=F32)


def dot3(left_high, left_low, right_ref):
    return (
        dot(left_high, right_ref[0]) + dot(left_high, right_ref[1]) + dot(left_low, right_ref[0])
    )


def kernel(
    shards,
    x_hbm,
    ct_hbm,
    f_hbm,
    first_hbm,
    last_hbm,
    inner_hbm,
    outer_hbm,
    twist_hbm,
    edge_hbm,
    gi_v,
    gf_v,
    x_v,
    f_v,
    first,
    last,
    inner,
    outer,
    twist,
    edge,
    x_out,
    x_got,
    f_out,
    f_got,
    g_out,
    g_got,
    y_out,
    y_got,
    wide,
    z_high,
    z_low,
    spec,
    f_wide,
    g_wide,
    w_high,
    w_low,
    back,
    y_wide,
    load_sem,
    send_sem,
    recv_sem,
    y_sem,
    plane_sem,
):
    width = LANES
    all_devices = 2 * shards
    points = 4 * shards * width
    both = 2 * OWN
    columns = shards // COLUMN
    planes = 2 * columns
    s, h = lax.axis_index("seq"), lax.axis_index("chan")
    own = h * shards + s
    spot, column = lax.rem(s, COLUMN), lax.div(s, COLUMN)
    place = 2 * column + h

    barrier = pltpu.get_barrier_semaphore()

    def in_column(k):
        return column * COLUMN + lax.rem(spot + k, COLUMN), h

    def in_plane(k):
        t = lax.rem(place + k, planes)
        return lax.div(t, 2) * COLUMN + spot, lax.rem(t, 2)

    def signal(semaphore, device):
        pl.semaphore_signal(semaphore, inc=1, device_id=device, device_id_type=MESH)

    for k in range(1, max(COLUMN, planes)):
        far = COLUMN // 2 + (k // 2 if k % 2 else -(k // 2))
        signal(barrier, in_column(far))
        if k < planes:
            far = planes // 2 + (k // 2 if k % 2 else -(k // 2))
            signal(barrier, in_plane(far))

    loads = [
        pltpu.make_async_copy(source, target, load_sem.at[at])
        for at, (source, target) in enumerate(
            (
                (x_hbm, x_v.at[0]),
                (ct_hbm, x_v.at[1]),
                (f_hbm, f_v),
                (first_hbm, first),
                (last_hbm, last),
                (inner_hbm, inner),
                (outer_hbm, outer),
                (twist_hbm, twist),
                (edge_hbm, edge),
            )
        )
    ]
    for load in loads:
        load.start()

    def remote(phase, source, target, device, arrival=None):
        return pltpu.make_async_remote_copy(
            src_ref=source,
            dst_ref=target,
            send_sem=send_sem.at[phase],
            recv_sem=recv_sem.at[phase] if arrival is None else arrival,
            device_id=device,
            device_id_type=MESH,
        )

    def to_column(phase, out, got, k, first_spot, arrival=None):
        t = lax.rem(place + k, planes)
        peer_h, start = lax.rem(t, 2), lax.div(t, 2) * COLUMN
        base = peer_h * shards + start
        for j in range(first_spot, COLUMN):
            at = lax.rem(spot + j, COLUMN)
            remote(phase, out.at[base + at], got.at[own], (start + at, peer_h), arrival).start()

    def to_row(phase, out, got, k, first_spot):
        start = lax.rem(column + k, columns) * COLUMN
        for j in range(first_spot, COLUMN):
            at = start + lax.rem(spot + j, COLUMN)
            remote(phase, out.at[at], got.at[s], (at, h)).start()

    def rest(count, step):
        def body(k, carry):
            step(k)
            return carry

        lax.fori_loop(1, count, body, 0)

    def whole(phase, out, got, count):
        some = pl.ds(0, count - 1)
        return remote(phase, out.at[some], got.at[some], in_plane(1))

    def turn_x(t):
        at = pl.ds(pl.multiple_of(t * LANES, LANES), LANES)
        parts = [x_v[a, :, at].astype(F32).T.reshape(LANES // OWN, OWN, width) for a in range(2)]
        x_out[pl.ds(t * (LANES // OWN), LANES // OWN)] = jnp.concatenate(parts, axis=1).astype(BF16)

    def turn_f(t):
        at = pl.ds(pl.multiple_of(t * LANES, LANES), LANES)
        for g in range(2):
            parts = [
                f_v[part, g, :, at].astype(F32).T.reshape(LANES // OWN, OWN, width)
                for part in range(2)
            ]
            f_out[pl.ds(t * (LANES // OWN), LANES // OWN), g] = jnp.concatenate(
                parts, axis=1
            ).astype(BF16)

    loads[0].wait()
    loads[1].wait()
    turn_x(h * columns + column)
    loads[2].wait()
    turn_f(column)
    rest(planes, lambda k: turn_x(lax.rem(h * columns + column + k, planes)))
    pl.semaphore_wait(barrier, COLUMN - 1 + planes - 1)
    for k in range(1, planes):
        signal(plane_sem, in_plane(k))
    to_column(0, x_out, x_got, 0, 1)
    to_row(1, f_out, f_got, 0, 1)
    rest(columns, lambda k: turn_f(lax.rem(column + k, columns)))
    x_got[own] = x_out[own]
    f_got[s] = f_out[s]
    pl.semaphore_wait(plane_sem, planes - 1)
    rest(planes, lambda k: to_column(0, x_out, x_got, k, 0))
    rest(columns, lambda k: to_row(1, f_out, f_got, k, 0))
    for load in loads[3:]:
        load.wait()

    whole(0, x_out, x_got, all_devices).wait_recv()

    def widen_x(t, carry):
        rows = pl.ds(pl.multiple_of(t * 16 * both, 16 * both), 16 * both)
        wide[rows] = x_got[pl.ds(t * 16, 16)].astype(F32).reshape(16 * both, width)
        return carry

    lax.fori_loop(0, all_devices // 16, widen_x, 0)

    def forward_first(q, carry):
        x = jnp.concatenate(
            [wide[pl.ds(a * shards * both + q, shards, stride=both), :] for a in range(2)], axis=1
        ).astype(BF16)
        y = dot(first[...], jnp.concatenate([x, x], axis=0))
        real, imag = y[:shards], y[shards:]
        alone = imag[0:1]
        zero_row = lax.broadcasted_iota(jnp.int32, imag.shape, 0) == 0
        imag = jnp.where(zero_row, 0.0, imag)
        z = jnp.concatenate(
            [real * twist[0] - imag * twist[1], real * twist[1] + imag * twist[0]], axis=1
        )
        rows = pl.ds(pl.multiple_of(q * shards, shards), shards)
        high, low = halves(z)
        z_high[rows] = high
        z_low[rows] = low
        spec[pl.ds(both * shards + q, 1), :] = jnp.concatenate(
            [alone * edge[0:1], alone * edge[1:2]], axis=1
        )
        return carry

    lax.fori_loop(0, both, forward_first, 0)
    tail = pl.ds(both * shards, both)
    high, low = halves(spec[tail])
    z_high[tail] = high
    z_low[tail] = low

    rows_forward = z_high.shape[0]
    step_forward = rows_forward // 3 if rows_forward % 48 == 0 else rows_forward

    def forward_second(t, carry):
        rows = pl.ds(pl.multiple_of(t * step_forward, 16), step_forward)
        spec[rows] = dot3(z_high[rows], z_low[rows], inner)
        return carry

    lax.fori_loop(0, rows_forward // step_forward, forward_second, 0)

    for q in range(both):
        zero, extra = pl.ds(q * shards, 1), pl.ds(both * shards + q, 1)
        kept = spec[zero, 2 * width : 3 * width]
        spec[zero, 2 * width :] = spec[extra, : 2 * width]
        spec[extra, 2 * width : 3 * width] = kept

    corner = (lax.broadcasted_iota(jnp.int32, (shards, width), 0) == 0) & (
        lax.broadcasted_iota(jnp.int32, (shards, width), 1) == 0
    )

    def spectrum(q, g):
        rows = pl.ds(pl.multiple_of(q * shards, shards), shards)
        at = 2 * width * g
        return spec[rows, at : at + width], spec[rows, at + width : at + 2 * width]

    def top(q):
        return spec[pl.ds(both * shards + q, 1), 3 * width - 1 : 3 * width]

    for ch in range(OWN):
        for g in range(2):
            (ur, ui), (vr, vi) = spectrum(ch, g), spectrum(OWN + ch, g)
            real = (ur * vr + ui * vi) * (2.0 / points)
            imag = (ur * vi - ui * vr) * (2.0 / points)
            if g == 0:
                real = jnp.where(corner, 0.5 * real, real)
                imag = jnp.where(corner, top(ch) * top(OWN + ch) * (1.0 / points), imag)
            g_wide[g, pl.ds(ch, shards, stride=both), :] = real
            g_wide[g, pl.ds(OWN + ch, shards, stride=both), :] = imag

    def narrow_g(t, carry):
        rows = pl.ds(pl.multiple_of(t * 16 * both, 16 * both), 16 * both)
        for g in range(2):
            g_out[pl.ds(t * 16, 16), g] = g_wide[g, rows].reshape(16, both, width).astype(BF16)
        return carry

    lax.fori_loop(0, shards // 16, narrow_g, 0)
    g_got[s] = g_out[s]
    rest(columns, lambda k: to_row(2, g_out, g_got, k, 0))
    to_row(2, g_out, g_got, 0, 1)

    whole(1, f_out, f_got, shards).wait_recv()

    def widen_f(t, carry):
        rows = pl.ds(pl.multiple_of(t * 16 * both, 16 * both), 16 * both)
        for g in range(2):
            f_wide[g, rows] = f_got[pl.ds(t * 16, 16), g].astype(F32).reshape(16 * both, width)
        return carry

    lax.fori_loop(0, shards // 16, widen_f, 0)

    row_at = lax.broadcasted_iota(jnp.int32, (shards, width), 0)
    lane_at = lax.broadcasted_iota(jnp.int32, (shards, width), 1)
    lane_one = lax.broadcasted_iota(jnp.int32, (1, width), 1)
    extra_rows = w_high.shape[0] - OWN * shards
    back[pl.ds(OWN * shards, extra_rows)] = jnp.zeros((extra_rows, 4 * width), F32)
    for ch in range(OWN):
        fields = []
        for g in range(2):
            vr, vi = spectrum(OWN + ch, g)
            fr = f_wide[g, pl.ds(ch, shards, stride=both), :]
            fi = f_wide[g, pl.ds(OWN + ch, shards, stride=both), :]
            if g == 0:
                above = top(OWN + ch) * fi[0:1, 0:1]
                fi = jnp.where(corner, 0.0, fi)
            fields.append((fr * vr + fi * vi, fr * vi - fi * vr))
        (ar, ai), (br, bi) = fields
        back[pl.ds(OWN * shards + ch, 1), : 2 * width] = 2.0 * jnp.concatenate(
            [br[0:1], bi[0:1]], axis=1
        )
        twice = (row_at == 0) & (lane_at > 0)
        ar = jnp.where(twice, 2.0 * ar, ar)
        ai = jnp.where(twice, 2.0 * ai, jnp.where(corner, 0.0, ai))
        br = jnp.where(row_at == 0, jnp.where(lane_one == width - 1, above, 0.0), br)
        bi = jnp.where(row_at == 0, 0.0, bi)
        high, low = halves(jnp.concatenate([ar, ai, br, bi], axis=1))
        rows = pl.ds(ch * shards, shards)
        w_high[rows] = high
        w_low[rows] = low
    tail_back = pl.ds(OWN * shards, extra_rows)
    high, low = halves(back[tail_back])
    w_high[tail_back] = high
    w_low[tail_back] = low

    rows_back = w_high.shape[0]
    step_back = rows_back // 3 if rows_back % 48 == 0 else rows_back

    def inverse_first(t, carry):
        rows = pl.ds(pl.multiple_of(t * step_back, 16), step_back)
        back[rows] = dot3(w_high[rows], w_low[rows], outer)
        return carry

    lax.fori_loop(0, rows_back // step_back, inverse_first, 0)

    for ch in range(OWN):
        rows = pl.ds(ch * shards, shards)
        hr, hi = back[rows, : 2 * width], back[rows, 2 * width :]
        extra = pl.ds(OWN * shards + ch, 1)
        er, ei = back[extra, : 2 * width], back[extra, 2 * width :]
        kr = hr * twist[0] + hi * twist[1]
        ki = hi * twist[0] - hr * twist[1]
        zero_row = lax.broadcasted_iota(jnp.int32, ki.shape, 0) == 0
        ki = jnp.where(zero_row, er * edge[0:1] + ei * edge[1:2], ki)
        high, low = halves(jnp.concatenate([kr, ki], axis=0))
        main = dot(last[...], high)
        y = main[:shards] + main[shards:] + dot(last[pl.ds(0, shards)], low)
        y = y * (1.0 / points)
        for a in range(2):
            y_wide[a, pl.ds(ch, shards, stride=OWN), :] = y[:, a * width : (a + 1) * width]

    def narrow_y(t, carry):
        rows = pl.ds(pl.multiple_of(t * 16 * OWN, 16 * OWN), 16 * OWN)
        for a in range(2):
            y_out[pl.ds(a * shards + t * 16, 16)] = (
                y_wide[a, rows].reshape(16, OWN, width).astype(BF16)
            )
        return carry

    lax.fori_loop(0, shards // 16, narrow_y, 0)
    y_got[own] = y_out[own]
    mine = h * columns + column

    def y_to(k, at):
        t = lax.rem(place + k, planes)
        peer_h, start = lax.rem(t, 2), lax.div(t, 2) * COLUMN
        remote(
            3, y_out.at[peer_h * shards + start + at], y_got.at[own], (start + at, peer_h), y_sem.at[mine]
        ).start()

    most = max(LEADS)

    def send_y(step, carry):
        for z, lead in enumerate(LEADS):
            m = step - (most - lead)

            @pl.when((m >= 0) & (m < planes))
            def _():
                k = lax.rem(m + 1, planes)
                for core in range(2):
                    at = 2 * z + core

                    @pl.when((k > 0) | (spot != at))
                    def _():
                        y_to(k, at)

        return carry

    lax.fori_loop(0, planes + most, send_y, 0)

    whole(2, g_out, g_got, shards).wait_recv()

    def turn_g(t, carry):
        at = pl.ds(pl.multiple_of(t * LANES, LANES), LANES)
        for g in range(2):
            block = g_got[pl.ds(t * (LANES // OWN), LANES // OWN), g].astype(F32)
            for part in range(2):
                rows = block[:, part * OWN : (part + 1) * OWN].reshape(LANES, width)
                gf_v[part, g, :, at] = rows.T.astype(BF16)
        return carry

    lax.fori_loop(0, shards * OWN // LANES, turn_g, 0)


    def turn_y(k, missing):
        t = lax.rem(place - k + planes, planes)
        t = lax.rem(t, 2) * columns + lax.div(t, 2)
        first_row = t * COLUMN
        some = pl.ds(first_row, COLUMN - missing)
        remote(3, y_out.at[some], y_got.at[some], in_plane(1), y_sem.at[t]).wait_recv()
        at = pl.ds(pl.multiple_of(t * LANES, LANES), LANES)
        rows = y_got[pl.ds(first_row, COLUMN)].astype(F32).reshape(LANES, width)
        gi_v[:, at] = rows.T.astype(BF16)

    rest(planes, lambda k: turn_y(k, 0))
    turn_y(0, 1)

    whole(0, x_out, x_got, all_devices).wait_send()
    whole(1, f_out, f_got, shards).wait_send()
    whole(2, g_out, g_got, shards).wait_send()
    whole(3, y_out, y_got, all_devices).wait_send()


def place(gi, gf, gi_hbm, gf_hbm, sem):
    first = pltpu.make_async_copy(gf, gf_hbm, sem.at[0])
    second = pltpu.make_async_copy(gi, gi_hbm, sem.at[1])
    first.start()
    second.start()
    first.wait()
    second.wait()


def local(inputs, cotangent, filter_spec):
    width, channels = inputs.shape
    shards = lax.axis_size("seq")
    group = channels // 2
    both = 2 * OWN
    constants = [jnp.asarray(table) for table in tables(shards, width)]
    extra = 32
    scratch = [
        ((2, width, channels), BF16),
        ((2, 2, width, group), BF16),
        *[(tuple(table.shape), table.dtype) for table in constants],
        ((2 * shards, both, width), BF16),
        ((2 * shards, both, width), BF16),
        ((shards, 2, both, width), BF16),
        ((shards, 2, both, width), BF16),
        ((shards, 2, both, width), BF16),
        ((shards, 2, both, width), BF16),
        ((2 * shards, OWN, width), BF16),
        ((2 * shards, OWN, width), BF16),
        ((2 * shards * both + both, width), F32),
        ((both * shards + both, 4 * width), BF16),
        ((both * shards + both, 4 * width), BF16),
        ((both * shards + both, 4 * width), F32),
        ((2, shards * both + both, width), F32),
        ((2, shards * both + both, width), F32),
        ((OWN * shards + extra, 4 * width), BF16),
        ((OWN * shards + extra, 4 * width), BF16),
        ((OWN * shards + extra, 4 * width), F32),
        ((2, shards * OWN + OWN, width), F32),
    ]
    gradients = pl.pallas_call(
        functools.partial(kernel, shards),
        out_shape=(
            pltpu.VMEM((width, channels), BF16),
            pltpu.VMEM((2, 2, width, group), BF16),
        ),
        in_specs=[pl.BlockSpec(memory_space=pl.ANY)] * 9,
        out_specs=[pl.BlockSpec(memory_space=pltpu.VMEM)] * 2,
        scratch_shapes=[pltpu.VMEM(shape, dtype) for shape, dtype in scratch]
        + [
            pltpu.SemaphoreType.DMA((9,)),
            pltpu.SemaphoreType.DMA((4,)),
            pltpu.SemaphoreType.DMA((3,)),
            pltpu.SemaphoreType.DMA((2 * shards // COLUMN,)),
            pltpu.SemaphoreType.REGULAR,
        ],
        compiler_params=pltpu.CompilerParams(
            collective_id=0, has_side_effects=True, vmem_limit_bytes=58 << 20
        ),
        name="hyena_backward",
    )(inputs, cotangent, filter_spec, *constants)
    return pl.pallas_call(
        place,
        out_shape=(
            pltpu.HBM((width, channels), BF16),
            pltpu.HBM((2, 2, width, group), BF16),
        ),
        in_specs=[pl.BlockSpec(memory_space=pltpu.VMEM)] * 2,
        out_specs=[pl.BlockSpec(memory_space=pl.ANY)] * 2,
        scratch_shapes=[pltpu.SemaphoreType.DMA((2,))],
        name="place",
    )(*[pltpu.with_memory_space_constraint(g, pltpu.VMEM) for g in gradients])


def solution(mesh):
    return jax.shard_map(
        local,
        mesh=mesh,
        in_specs=(P(("seq", "chan"), None), P(("seq", "chan"), None), P(None, "seq", None, "chan")),
        out_specs=(P(("seq", "chan"), None), P(None, "seq", None, "chan")),
        check_vma=False,
    )
```

```python
import functools

import jax
import jax.numpy as jnp
import ml_dtypes
import numpy as np
from jax import lax
from jax.experimental import pallas as pl
from jax.experimental.pallas import tpu as pltpu
from jax.sharding import PartitionSpec as P

MESH = pl.DeviceIdType.MESH
OWN = 8
LANES = 128
COLUMN = 16
TURNS = (0, 1, 15, 2, 14, 3, 13, 4, 12, 5, 11, 6, 10, 7, 9, 8)
LEADS = (8, 6, 5, 3, 0, 0, 0, 0)
F32 = jnp.float32
BF16 = jnp.bfloat16


def split(table):
    high = table.astype(ml_dtypes.bfloat16)
    low = (table - high.astype(np.float64)).astype(ml_dtypes.bfloat16)
    return high, low


def angles(left, right, modulus):
    return 2.0 * np.pi * (np.outer(left, right) % modulus) / modulus


@functools.cache
def tables(shards, width):
    classes, offsets = 2 * shards, 2 * width
    points = classes * offsets
    c = np.arange(shards)
    p = np.arange(shards)
    j = np.arange(offsets)
    r = np.arange(width)
    turn = angles(c, p, classes)
    first = np.concatenate([np.cos(turn), -np.sin(turn)])
    first[shards] = np.cos(np.pi * p)
    last = np.concatenate([2.0 * np.cos(turn.T), -2.0 * np.sin(turn.T)], axis=1)
    last[:, 0] = 1.0
    last[:, shards] = np.cos(np.pi * p)
    twist = angles(np.arange(shards + 1), j, points)
    twist_cos, twist_sin = np.cos(twist), -np.sin(twist)
    low, up = angles(j, r, offsets), angles(j, r + 1, offsets)
    inner = np.block(
        [
            [np.cos(low), -np.sin(low), np.cos(up), -np.sin(up)],
            [np.sin(low), np.cos(low), -np.sin(up), -np.cos(up)],
        ]
    )
    edge = np.stack([twist_cos[shards], twist_sin[shards]] + [np.zeros(offsets)] * 6)
    first_high, first_low = split(first)
    last_high, last_low = split(last)
    inner_high, inner_low = split(inner)
    return (
        np.concatenate([first_high, first_low], axis=1),
        np.concatenate([last_high, last_low], axis=0),
        np.stack([inner_high, inner_low]),
        np.stack([inner_high.T, inner_low.T]),
        np.stack([twist_cos[:shards], twist_sin[:shards]]).astype(np.float32),
        edge.astype(np.float32),
    )


def halves(value):
    high = value.astype(BF16)
    return high, (value - high.astype(F32)).astype(BF16)


def dot(left, right):
    return jnp.dot(left, right, preferred_element_type=F32)


def dot3(left_high, left_low, right_ref):
    return (
        dot(left_high, right_ref[0]) + dot(left_high, right_ref[1]) + dot(left_low, right_ref[0])
    )


def kernel(
    shards,
    x_hbm,
    ct_hbm,
    f_hbm,
    first_hbm,
    last_hbm,
    inner_hbm,
    outer_hbm,
    twist_hbm,
    edge_hbm,
    gi_v,
    gf_v,
    x_v,
    f_v,
    first,
    last,
    inner,
    outer,
    twist,
    edge,
    x_out,
    x_got,
    f_out,
    f_got,
    g_out,
    g_got,
    y_out,
    y_got,
    wide,
    z_high,
    z_low,
    spec,
    f_wide,
    g_wide,
    w_high,
    w_low,
    back,
    y_wide,
    load_sem,
    send_sem,
    recv_sem,
    y_sem,
    plane_sem,
):
    width = LANES
    all_devices = 2 * shards
    points = 4 * shards * width
    both = 2 * OWN
    columns = shards // COLUMN
    planes = 2 * columns
    s, h = lax.axis_index("seq"), lax.axis_index("chan")
    own = h * shards + s
    spot, column = lax.rem(s, COLUMN), lax.div(s, COLUMN)
    place = 2 * column + h

    barrier = pltpu.get_barrier_semaphore()

    def in_column(k):
        return column * COLUMN + lax.rem(spot + k, COLUMN), h

    def in_plane(k):
        t = lax.rem(place + k, planes)
        return lax.div(t, 2) * COLUMN + spot, lax.rem(t, 2)

    def signal(semaphore, device):
        pl.semaphore_signal(semaphore, inc=1, device_id=device, device_id_type=MESH)

    for k in range(1, max(COLUMN, planes)):
        far = COLUMN // 2 + (k // 2 if k % 2 else -(k // 2))
        signal(barrier, in_column(far))
        if k < planes:
            far = planes // 2 + (k // 2 if k % 2 else -(k // 2))
            signal(barrier, in_plane(far))

    loads = [
        pltpu.make_async_copy(source, target, load_sem.at[at])
        for at, (source, target) in enumerate(
            (
                (x_hbm, x_v.at[0]),
                (ct_hbm, x_v.at[1]),
                (f_hbm, f_v),
                (first_hbm, first),
                (last_hbm, last),
                (inner_hbm, inner),
                (outer_hbm, outer),
                (twist_hbm, twist),
                (edge_hbm, edge),
            )
        )
    ]
    for load in loads:
        load.start()

    def remote(phase, source, target, device, arrival=None):
        return pltpu.make_async_remote_copy(
            src_ref=source,
            dst_ref=target,
            send_sem=send_sem.at[phase],
            recv_sem=recv_sem.at[phase] if arrival is None else arrival,
            device_id=device,
            device_id_type=MESH,
        )

    def to_column(phase, out, got, k, first_spot, arrival=None):
        t = lax.rem(place + k, planes)
        peer_h, start = lax.rem(t, 2), lax.div(t, 2) * COLUMN
        base = peer_h * shards + start
        for j in TURNS[first_spot:]:
            at = lax.rem(spot + j, COLUMN)
            remote(phase, out.at[base + at], got.at[own], (start + at, peer_h), arrival).start()

    def to_row(phase, out, got, k, first_spot):
        start = lax.rem(column + k, columns) * COLUMN
        for j in TURNS[first_spot:]:
            at = start + lax.rem(spot + j, COLUMN)
            remote(phase, out.at[at], got.at[s], (at, h)).start()

    def rest(count, step):
        def body(k, carry):
            step(k)
            return carry

        lax.fori_loop(1, count, body, 0)

    def whole(phase, out, got, count):
        some = pl.ds(0, count - 1)
        return remote(phase, out.at[some], got.at[some], in_plane(1))

    def turn_x(t):
        at = pl.ds(pl.multiple_of(t * LANES, LANES), LANES)
        parts = [x_v[a, :, at].astype(F32).T.reshape(LANES // OWN, OWN, width) for a in range(2)]
        x_out[pl.ds(t * (LANES // OWN), LANES // OWN)] = jnp.concatenate(parts, axis=1).astype(BF16)

    def turn_f(t):
        at = pl.ds(pl.multiple_of(t * LANES, LANES), LANES)
        for g in range(2):
            parts = [
                f_v[part, g, :, at].astype(F32).T.reshape(LANES // OWN, OWN, width)
                for part in range(2)
            ]
            f_out[pl.ds(t * (LANES // OWN), LANES // OWN), g] = jnp.concatenate(
                parts, axis=1
            ).astype(BF16)

    loads[0].wait()
    loads[1].wait()
    turn_x(h * columns + column)
    loads[2].wait()
    turn_f(column)
    rest(planes, lambda k: turn_x(lax.rem(h * columns + column + k, planes)))
    pl.semaphore_wait(barrier, COLUMN - 1 + planes - 1)
    for k in range(1, planes):
        signal(plane_sem, in_plane(k))
    to_column(0, x_out, x_got, 0, 1)
    to_row(1, f_out, f_got, 0, 1)
    rest(columns, lambda k: turn_f(lax.rem(column + k, columns)))
    x_got[own] = x_out[own]
    f_got[s] = f_out[s]
    pl.semaphore_wait(plane_sem, planes - 1)
    rest(planes, lambda k: to_column(0, x_out, x_got, k, 0))
    rest(columns, lambda k: to_row(1, f_out, f_got, k, 0))
    for load in loads[3:]:
        load.wait()

    whole(0, x_out, x_got, all_devices).wait_recv()

    def widen_x(t, carry):
        rows = pl.ds(pl.multiple_of(t * 16 * both, 16 * both), 16 * both)
        wide[rows] = x_got[pl.ds(t * 16, 16)].astype(F32).reshape(16 * both, width)
        return carry

    lax.fori_loop(0, all_devices // 16, widen_x, 0)

    def forward_first(q, carry):
        x = jnp.concatenate(
            [wide[pl.ds(a * shards * both + q, shards, stride=both), :] for a in range(2)], axis=1
        ).astype(BF16)
        y = dot(first[...], jnp.concatenate([x, x], axis=0))
        real, imag = y[:shards], y[shards:]
        alone = imag[0:1]
        zero_row = lax.broadcasted_iota(jnp.int32, imag.shape, 0) == 0
        imag = jnp.where(zero_row, 0.0, imag)
        z = jnp.concatenate(
            [real * twist[0] - imag * twist[1], real * twist[1] + imag * twist[0]], axis=1
        )
        rows = pl.ds(pl.multiple_of(q * shards, shards), shards)
        high, low = halves(z)
        z_high[rows] = high
        z_low[rows] = low
        spec[pl.ds(both * shards + q, 1), :] = jnp.concatenate(
            [alone * edge[0:1], alone * edge[1:2]], axis=1
        )
        return carry

    lax.fori_loop(0, both, forward_first, 0)
    tail = pl.ds(both * shards, both)
    high, low = halves(spec[tail])
    z_high[tail] = high
    z_low[tail] = low

    rows_forward = z_high.shape[0]
    step_forward = rows_forward // 3 if rows_forward % 48 == 0 else rows_forward

    def forward_second(t, carry):
        rows = pl.ds(pl.multiple_of(t * step_forward, 16), step_forward)
        spec[rows] = dot3(z_high[rows], z_low[rows], inner)
        return carry

    lax.fori_loop(0, rows_forward // step_forward, forward_second, 0)

    for q in range(both):
        zero, extra = pl.ds(q * shards, 1), pl.ds(both * shards + q, 1)
        kept = spec[zero, 2 * width : 3 * width]
        spec[zero, 2 * width :] = spec[extra, : 2 * width]
        spec[extra, 2 * width : 3 * width] = kept

    corner = (lax.broadcasted_iota(jnp.int32, (shards, width), 0) == 0) & (
        lax.broadcasted_iota(jnp.int32, (shards, width), 1) == 0
    )

    def spectrum(q, g):
        rows = pl.ds(pl.multiple_of(q * shards, shards), shards)
        at = 2 * width * g
        return spec[rows, at : at + width], spec[rows, at + width : at + 2 * width]

    def top(q):
        return spec[pl.ds(both * shards + q, 1), 3 * width - 1 : 3 * width]

    for ch in range(OWN):
        for g in range(2):
            (ur, ui), (vr, vi) = spectrum(ch, g), spectrum(OWN + ch, g)
            real = (ur * vr + ui * vi) * (2.0 / points)
            imag = (ur * vi - ui * vr) * (2.0 / points)
            if g == 0:
                real = jnp.where(corner, 0.5 * real, real)
                imag = jnp.where(corner, top(ch) * top(OWN + ch) * (1.0 / points), imag)
            g_wide[g, pl.ds(ch, shards, stride=both), :] = real
            g_wide[g, pl.ds(OWN + ch, shards, stride=both), :] = imag

    def narrow_g(t, carry):
        rows = pl.ds(pl.multiple_of(t * 16 * both, 16 * both), 16 * both)
        for g in range(2):
            g_out[pl.ds(t * 16, 16), g] = g_wide[g, rows].reshape(16, both, width).astype(BF16)
        return carry

    lax.fori_loop(0, shards // 16, narrow_g, 0)
    g_got[s] = g_out[s]
    rest(columns, lambda k: to_row(2, g_out, g_got, k, 0))
    to_row(2, g_out, g_got, 0, 1)

    whole(1, f_out, f_got, shards).wait_recv()

    def widen_f(t, carry):
        rows = pl.ds(pl.multiple_of(t * 16 * both, 16 * both), 16 * both)
        for g in range(2):
            f_wide[g, rows] = f_got[pl.ds(t * 16, 16), g].astype(F32).reshape(16 * both, width)
        return carry

    lax.fori_loop(0, shards // 16, widen_f, 0)

    row_at = lax.broadcasted_iota(jnp.int32, (shards, width), 0)
    lane_at = lax.broadcasted_iota(jnp.int32, (shards, width), 1)
    lane_one = lax.broadcasted_iota(jnp.int32, (1, width), 1)
    extra_rows = w_high.shape[0] - OWN * shards
    back[pl.ds(OWN * shards, extra_rows)] = jnp.zeros((extra_rows, 4 * width), F32)
    for ch in range(OWN):
        fields = []
        for g in range(2):
            vr, vi = spectrum(OWN + ch, g)
            fr = f_wide[g, pl.ds(ch, shards, stride=both), :]
            fi = f_wide[g, pl.ds(OWN + ch, shards, stride=both), :]
            if g == 0:
                above = top(OWN + ch) * fi[0:1, 0:1]
                fi = jnp.where(corner, 0.0, fi)
            fields.append((fr * vr + fi * vi, fr * vi - fi * vr))
        (ar, ai), (br, bi) = fields
        back[pl.ds(OWN * shards + ch, 1), : 2 * width] = 2.0 * jnp.concatenate(
            [br[0:1], bi[0:1]], axis=1
        )
        twice = (row_at == 0) & (lane_at > 0)
        ar = jnp.where(twice, 2.0 * ar, ar)
        ai = jnp.where(twice, 2.0 * ai, jnp.where(corner, 0.0, ai))
        br = jnp.where(row_at == 0, jnp.where(lane_one == width - 1, above, 0.0), br)
        bi = jnp.where(row_at == 0, 0.0, bi)
        high, low = halves(jnp.concatenate([ar, ai, br, bi], axis=1))
        rows = pl.ds(ch * shards, shards)
        w_high[rows] = high
        w_low[rows] = low
    tail_back = pl.ds(OWN * shards, extra_rows)
    high, low = halves(back[tail_back])
    w_high[tail_back] = high
    w_low[tail_back] = low

    rows_back = w_high.shape[0]
    step_back = rows_back // 3 if rows_back % 48 == 0 else rows_back

    def inverse_first(t, carry):
        rows = pl.ds(pl.multiple_of(t * step_back, 16), step_back)
        back[rows] = dot3(w_high[rows], w_low[rows], outer)
        return carry

    lax.fori_loop(0, rows_back // step_back, inverse_first, 0)

    for ch in range(OWN):
        rows = pl.ds(ch * shards, shards)
        hr, hi = back[rows, : 2 * width], back[rows, 2 * width :]
        extra = pl.ds(OWN * shards + ch, 1)
        er, ei = back[extra, : 2 * width], back[extra, 2 * width :]
        kr = hr * twist[0] + hi * twist[1]
        ki = hi * twist[0] - hr * twist[1]
        zero_row = lax.broadcasted_iota(jnp.int32, ki.shape, 0) == 0
        ki = jnp.where(zero_row, er * edge[0:1] + ei * edge[1:2], ki)
        high, low = halves(jnp.concatenate([kr, ki], axis=0))
        main = dot(last[...], high)
        y = main[:shards] + main[shards:] + dot(last[pl.ds(0, shards)], low)
        y = y * (1.0 / points)
        for a in range(2):
            y_wide[a, pl.ds(ch, shards, stride=OWN), :] = y[:, a * width : (a + 1) * width]

    def narrow_y(t, carry):
        rows = pl.ds(pl.multiple_of(t * 16 * OWN, 16 * OWN), 16 * OWN)
        for a in range(2):
            y_out[pl.ds(a * shards + t * 16, 16)] = (
                y_wide[a, rows].reshape(16, OWN, width).astype(BF16)
            )
        return carry

    lax.fori_loop(0, shards // 16, narrow_y, 0)
    y_got[own] = y_out[own]
    mine = h * columns + column

    def y_to(k, at):
        t = lax.rem(place + k, planes)
        peer_h, start = lax.rem(t, 2), lax.div(t, 2) * COLUMN
        remote(
            3, y_out.at[peer_h * shards + start + at], y_got.at[own], (start + at, peer_h), y_sem.at[mine]
        ).start()

    most = max(LEADS)

    def send_y(step, carry):
        for z, lead in enumerate(LEADS):
            m = step - (most - lead)

            @pl.when((m >= 0) & (m < planes))
            def _():
                k = lax.rem(m + 1, planes)
                for core in range(2):
                    at = 2 * z + core

                    @pl.when((k > 0) | (spot != at))
                    def _():
                        y_to(k, at)

        return carry

    lax.fori_loop(0, planes + most, send_y, 0)

    whole(2, g_out, g_got, shards).wait_recv()

    def turn_g(t, carry):
        at = pl.ds(pl.multiple_of(t * LANES, LANES), LANES)
        for g in range(2):
            block = g_got[pl.ds(t * (LANES // OWN), LANES // OWN), g].astype(F32)
            for part in range(2):
                rows = block[:, part * OWN : (part + 1) * OWN].reshape(LANES, width)
                gf_v[part, g, :, at] = rows.T.astype(BF16)
        return carry

    lax.fori_loop(0, shards * OWN // LANES, turn_g, 0)


    def turn_y(k, missing):
        t = lax.rem(place - k + planes, planes)
        t = lax.rem(t, 2) * columns + lax.div(t, 2)
        first_row = t * COLUMN
        some = pl.ds(first_row, COLUMN - missing)
        remote(3, y_out.at[some], y_got.at[some], in_plane(1), y_sem.at[t]).wait_recv()
        at = pl.ds(pl.multiple_of(t * LANES, LANES), LANES)
        rows = y_got[pl.ds(first_row, COLUMN)].astype(F32).reshape(LANES, width)
        gi_v[:, at] = rows.T.astype(BF16)

    rest(planes, lambda k: turn_y(k, 0))
    turn_y(0, 1)

    whole(0, x_out, x_got, all_devices).wait_send()
    whole(1, f_out, f_got, shards).wait_send()
    whole(2, g_out, g_got, shards).wait_send()
    whole(3, y_out, y_got, all_devices).wait_send()


def place(gi, gf, gi_hbm, gf_hbm, sem):
    first = pltpu.make_async_copy(gf, gf_hbm, sem.at[0])
    second = pltpu.make_async_copy(gi, gi_hbm, sem.at[1])
    first.start()
    second.start()
    first.wait()
    second.wait()


def local(inputs, cotangent, filter_spec):
    width, channels = inputs.shape
    shards = lax.axis_size("seq")
    group = channels // 2
    both = 2 * OWN
    constants = [jnp.asarray(table) for table in tables(shards, width)]
    extra = 32
    scratch = [
        ((2, width, channels), BF16),
        ((2, 2, width, group), BF16),
        *[(tuple(table.shape), table.dtype) for table in constants],
        ((2 * shards, both, width), BF16),
        ((2 * shards, both, width), BF16),
        ((shards, 2, both, width), BF16),
        ((shards, 2, both, width), BF16),
        ((shards, 2, both, width), BF16),
        ((shards, 2, both, width), BF16),
        ((2 * shards, OWN, width), BF16),
        ((2 * shards, OWN, width), BF16),
        ((2 * shards * both + both, width), F32),
        ((both * shards + both, 4 * width), BF16),
        ((both * shards + both, 4 * width), BF16),
        ((both * shards + both, 4 * width), F32),
        ((2, shards * both + both, width), F32),
        ((2, shards * both + both, width), F32),
        ((OWN * shards + extra, 4 * width), BF16),
        ((OWN * shards + extra, 4 * width), BF16),
        ((OWN * shards + extra, 4 * width), F32),
        ((2, shards * OWN + OWN, width), F32),
    ]
    gradients = pl.pallas_call(
        functools.partial(kernel, shards),
        out_shape=(
            pltpu.VMEM((width, channels), BF16),
            pltpu.VMEM((2, 2, width, group), BF16),
        ),
        in_specs=[pl.BlockSpec(memory_space=pl.ANY)] * 9,
        out_specs=[pl.BlockSpec(memory_space=pltpu.VMEM)] * 2,
        scratch_shapes=[pltpu.VMEM(shape, dtype) for shape, dtype in scratch]
        + [
            pltpu.SemaphoreType.DMA((9,)),
            pltpu.SemaphoreType.DMA((4,)),
            pltpu.SemaphoreType.DMA((3,)),
            pltpu.SemaphoreType.DMA((2 * shards // COLUMN,)),
            pltpu.SemaphoreType.REGULAR,
        ],
        compiler_params=pltpu.CompilerParams(
            collective_id=0, has_side_effects=True, vmem_limit_bytes=58 << 20
        ),
        name="hyena_backward",
    )(inputs, cotangent, filter_spec, *constants)
    return pl.pallas_call(
        place,
        out_shape=(
            pltpu.HBM((width, channels), BF16),
            pltpu.HBM((2, 2, width, group), BF16),
        ),
        in_specs=[pl.BlockSpec(memory_space=pltpu.VMEM)] * 2,
        out_specs=[pl.BlockSpec(memory_space=pl.ANY)] * 2,
        scratch_shapes=[pltpu.SemaphoreType.DMA((2,))],
        name="place",
    )(*[pltpu.with_memory_space_constraint(g, pltpu.VMEM) for g in gradients])


def solution(mesh):
    return jax.shard_map(
        local,
        mesh=mesh,
        in_specs=(P(("seq", "chan"), None), P(("seq", "chan"), None), P(None, "seq", None, "chan")),
        out_specs=(P(("seq", "chan"), None), P(None, "seq", None, "chan")),
        check_vma=False,
    )
```
